256 devices in a mesh: vid: 32 (over y, z_lo, core), aud: 2 (over z_hi), head: 4 (over x).
Axes of the slice: x: 4, y: 4, z: 8 (z_hi: 2, z_lo: 4; z = z_hi * 4 + z_lo), core: 2. Of those that a mesh axis runs over, the one named last changes fastest.
Arguments:
- video_query: bfloat16 [16384, 3072], P('vid', 'head'), may hold values from -9 to 9
- video_key_array: bfloat16 [16384, 3072], P('vid', 'head'), may hold values from -16 to 16
- video_value: bfloat16 [16384, 3072], P('vid', 'head'), may hold values from -6 to 6
- video_cotangent: bfloat16 [16384, 3072], P('vid', 'head'), may hold values from -6 to 6
- audio_query: bfloat16 [1024, 3072], P('aud', 'head'), may hold values from -9 to 9
- audio_key: bfloat16 [1024, 3072], P('aud', 'head'), may hold values from -16 to 16
- audio_value: bfloat16 [1024, 3072], P('aud', 'head'), may hold values from -6 to 6
- audio_cotangent: bfloat16 [1024, 3072], P('aud', 'head'), may hold values from -6 to 6
- alignment: int32 [128, 16], replicated, may hold values from 0 to 1, as said below
Outputs:
- grad_video_query: bfloat16 [16384, 3072], P('vid', 'head')
- grad_video_key: bfloat16 [16384, 3072], P('vid', 'head')
- grad_video_value: bfloat16 [16384, 3072], P('vid', 'head')
- grad_audio_query: bfloat16 [1024, 3072], P('aud', 'head')
- grad_audio_key: bfloat16 [1024, 3072], P('aud', 'head')
- grad_audio_value: bfloat16 [1024, 3072], P('aud', 'head')
The draws below stay inside these ranges and needn't reach their ends.
Inputs may be any that keep to these rules, and one draw needn't show every extreme that they name: `alignment`: each video time block i allows a contiguous run of audio time blocks that contains block c = 16 * i // 128 and lies within blocks c - 3 to c + 3; some video block allows all seven of c - 3 to c + 3.
All inputs are finite; a program needn't handle non-finite values.
Results may differ from the reference program's by a relative error of at most 0.006.
Values may be sent and summed in bfloat16 or wider, within the bound.
No kernel may reach another device: no remote copies, remote signals or barrier semaphores. Data moves between devices by JAX's collectives and lax.ppermute only.
A program may use at most 128 MiB of HBM per device.

```python
import jax
import jax.numpy as jnp
from jax import lax

HEADS = 24
DH = 128
VBLK = 128
ABLK = 64
D = 3072
NV = 16384
NA = 1024
NVB = 128
NAB = 16


def query_rows(key, rows, own):
    key = jax.random.fold_in(key, own)
    first, second = jax.random.split(key)
    base = jax.random.truncated_normal(first, -4.0, 4.0, (rows, D), jnp.float32)
    scales = jnp.exp(jax.random.uniform(second, (rows, 1), jnp.float32, jnp.log(0.5), jnp.log(1.5)))
    values = base * scales
    return values.astype(jnp.bfloat16)


def key_rows(key, rows, own):
    key = jax.random.fold_in(key, own)
    first, second = jax.random.split(key, 2)
    base = jax.random.truncated_normal(first, -4.0, 4.0, (rows, D), jnp.float32)
    scales = jnp.exp(jax.random.uniform(second, (rows, 1), jnp.float32, jnp.log(0.32), jnp.log(3.2)))
    values = base * scales
    return values.astype(jnp.bfloat16)


def draw_video_query(key, part):
    return query_rows(key, NV, 1)


def draw_audio_key(key, part):
    return key_rows(key, NA, 2)


def draw_audio_query(key, part):
    return query_rows(key, NA, 3)


def draw_video_key_array(key, part):
    return key_rows(key, NV, 4)


def draw_alignment(key, part):
    key = jax.random.fold_in(key, 11)
    reach = jax.random.randint(key, (NVB, 1), 0, 4)
    rows = jnp.arange(NVB)[:, None]
    reach = jnp.where(rows == NVB // 2, 3, reach)
    center = rows * NAB // NVB
    columns = jnp.arange(NAB)[None, :]
    return (jnp.abs(columns - center) <= reach).astype(jnp.int32)


def level_of(stream_key, dims, cuts, low, high):
    factor_of, own = 1.0, jax.random.fold_in(stream_key, 6)
    for dim, shards_of in cuts:
        steps = jnp.exp(jax.random.uniform(jax.random.fold_in(own, dim), (shards_of,), jnp.float32, low / len(cuts), high / len(cuts)))
        factor_of = factor_of * jnp.repeat(steps, dims[dim] // shards_of).reshape([-1 if axis == dim else 1 for axis in range(len(dims))])
    return factor_of


def centred(stream_key, dims, scale, most, pieces=(), dtype=jnp.bfloat16):
    values = scale * jax.random.normal(stream_key, dims, jnp.float32)
    if pieces:
        values = values * level_of(stream_key, dims, pieces, -0.22, 0.18)
    return jnp.clip(values, -most, most).astype(dtype)


def setup_inputs(seed: int = 0) -> dict:
    key_of = jax.random.split(jax.random.key(seed), 10)
    video_query = draw_video_query(jax.random.fold_in(key_of[9], 71), 0)
    video_key_array = draw_video_key_array(jax.random.fold_in(key_of[9], 71), 0)
    video_value = centred(key_of[2], (NV, D), 1.0, 6.0, ((0, 32), (1, 4)))
    video_cotangent = centred(key_of[3], (NV, D), 1.0, 6.0, ((0, 32), (1, 4)))
    audio_query = draw_audio_query(jax.random.fold_in(key_of[9], 71), 0)
    audio_key = draw_audio_key(jax.random.fold_in(key_of[9], 71), 0)
    audio_value = centred(key_of[6], (NA, D), 1.0, 6.0, ((0, 2), (1, 4)))
    audio_cotangent = centred(key_of[7], (NA, D), 1.0, 6.0, ((0, 2), (1, 4)))
    alignment = draw_alignment(jax.random.fold_in(key_of[9], 71), 0)
    return dict(video_query=video_query, video_key_array=video_key_array, video_value=video_value, video_cotangent=video_cotangent, audio_query=audio_query, audio_key=audio_key, audio_value=audio_value, audio_cotangent=audio_cotangent, alignment=alignment)


NEG = -1e30


def attention_backward(query, keys, values, cotangent, mask):
    scale = DH ** -0.5
    scores = jnp.dot(query, keys.T, preferred_element_type=jnp.float32) * scale
    scores = jnp.where(mask, scores, NEG)
    top = jnp.max(scores, axis=1, keepdims=True)
    weights = jnp.where(mask, jnp.exp(scores - top), 0.0)
    total = jnp.sum(weights, axis=1, keepdims=True)
    prob = weights / total
    dprob = jnp.dot(cotangent, values.T, preferred_element_type=jnp.float32)
    delta = jnp.sum(prob * dprob, axis=1, keepdims=True)
    dscore = (prob * (dprob - delta) * scale).astype(jnp.bfloat16)
    grad_query = jnp.dot(dscore, keys, preferred_element_type=jnp.float32)
    grad_keys = jnp.dot(dscore.T, query, preferred_element_type=jnp.float32)
    grad_values = jnp.dot(prob.astype(jnp.bfloat16).T, cotangent, preferred_element_type=jnp.float32)
    return grad_query, grad_keys, grad_values


def heads_first(array):
    return array.reshape(array.shape[0], HEADS, DH).transpose(1, 0, 2)


def heads_back(array):
    return array.transpose(1, 0, 2).reshape(array.shape[1], HEADS * DH).astype(jnp.bfloat16)


def reference(video_query, video_key_array, video_value, video_cotangent, audio_query, audio_key, audio_value, audio_cotangent, alignment):
    allowed = jnp.repeat(jnp.repeat(alignment, VBLK, axis=0), ABLK, axis=1) > 0
    reversed_direction = allowed.T

    def one_head(input_tensors):
        video_query_rows, video_key_rows, video_value_rows, video_gradient_set, audio_query_rows, audio_key_rows, audio_value_rows, audio_gradient_set = input_tensors
        dvq, dak, dav = attention_backward(video_query_rows, audio_key_rows, audio_value_rows, video_gradient_set, allowed)
        audio_query_gradient, video_key_gradient, video_value_gradient = attention_backward(audio_query_rows, video_key_rows, video_value_rows, audio_gradient_set, reversed_direction)
        return dvq, video_key_gradient, video_value_gradient, audio_query_gradient, dak, dav

    stacked = tuple(heads_first(x) for x in (video_query, video_key_array, video_value, video_cotangent, audio_query, audio_key, audio_value, audio_cotangent))
    dvq, video_key_gradient, video_value_gradient, audio_query_gradient, dak, dav = lax.map(one_head, stacked)
    return (heads_back(dvq), heads_back(video_key_gradient), heads_back(video_value_gradient), heads_back(audio_query_gradient), heads_back(dak), heads_back(dav))
```

```python
import functools
import math

import jax
import jax.numpy as jnp
from jax import lax
from jax.experimental import pallas as pl
from jax.experimental.pallas import tpu as pltpu
from jax.sharding import Mesh
from jax.sharding import PartitionSpec as P

DH = 128
VBLK = 128
ABLK = 64
NH = 6
HALF = 3
ROWS = 512
CH = 256
SCALE = DH ** -0.5
C2 = SCALE * math.log2(math.e)
MASKED = -1e30
FLOOR = -1e29
WIDE = HALF * DH
PAIRS = 6 * 2 * 512 * 512 * 128
F32 = jnp.float32
BF16 = jnp.bfloat16
STAT = ((3, 8, ROWS), F32)
BOTH = ((2, 8, ROWS), F32)

S_Y, S_Z, S_CORE, S_AUD, S_MASK = 0, 1, 2, 3, 4

MIB = 1024 * 1024


def limit(mib):
    return pltpu.CompilerParams(vmem_limit_bytes=mib * MIB)


def call(kernel, ins, outs, scratch, mib, flops, size, name, scal, *arrays):
    vmem = pl.BlockSpec(memory_space=pltpu.VMEM)
    return pl.pallas_call(
        kernel,
        in_specs=[pl.BlockSpec(memory_space=pltpu.SMEM)] + [vmem] * ins,
        out_specs=[vmem] * len(outs),
        out_shape=[jax.ShapeDtypeStruct(shape, dtype) for shape, dtype in outs],
        scratch_shapes=scratch,
        compiler_params=limit(mib),
        cost_estimate=pl.CostEstimate(flops=flops, bytes_accessed=size, transcendentals=0),
        name=name,
    )(scal, *arrays)


def dot_nt(a, b):
    return lax.dot_general(a, b, (((1,), (1,)), ((), ())), preferred_element_type=F32)


def dot_nn(a, b):
    return lax.dot_general(a, b, (((1,), (0,)), ((), ())), preferred_element_type=F32)


def bias_of(scal, half, i, j):
    return jnp.where(scal[S_MASK + i * 16 + half * 8 + j] > 0, 0.0, MASKED)


def chunk_active(scal, half, q):
    c = scal[S_Y] * 4 + scal[S_Z]
    first = half * 8 + q * (CH // ABLK)
    return jnp.logical_and(first <= c + 3, first + CH // ABLK - 1 >= c - 3)


def pair_bias(scal, half, i, j):
    lane = lax.broadcasted_iota(jnp.int32, (1, 128), 1)
    return jnp.where(lane < ABLK, bias_of(scal, half, i, j), bias_of(scal, half, i, j + 1))


def head_cols(g, r):
    if isinstance(g, int):
        return slice(g * WIDE + r * DH, g * WIDE + (r + 1) * DH)
    return pl.ds(pl.multiple_of(g * WIDE + r * DH, DH), DH)


def first_rows(held):
    for h in range(NH):
        held[h, 0:1, :] = jnp.full((1, ROWS), FLOOR, F32)
        held[h, 1:2, :] = jnp.zeros((1, ROWS), F32)
        held[h, 2:3, :] = jnp.zeros((1, ROWS), F32)


def store_rows(stat, held):
    for k in range(3):
        for h in range(NH):
            stat[k, h : h + 1, :] = held[h, k : k + 1, :]
        stat[k, NH:8, :] = jnp.ones((8 - NH, ROWS), F32)


def audio_stats_kernel(scal, vk, vv, aq, ag, stat, held):
    half = scal[S_AUD]
    first_rows(held)
    for q in range(ROWS // CH):

        @pl.when(chunk_active(scal, half, q))
        def _():
            rows = slice(q * CH, (q + 1) * CH)
            bias = [[pair_bias(scal, half, i, q * 4 + jj * 2) for i in range(4)] for jj in range(2)]
            for h in range(NH):
                hc = head_cols(0, h)
                s = dot_nt(vk[:, hc], aq[rows, hc])
                t = dot_nt(vv[:, hc], ag[rows, hc])
                for jj in range(CH // 128):
                    cols = slice(jj * 128, (jj + 1) * 128)
                    out = slice(q * CH + jj * 128, q * CH + jj * 128 + 128)
                    top = jnp.full((1, 128), FLOOR, F32)
                    for i in range(4):
                        best = jnp.max(s[i * 128 : (i + 1) * 128, cols], axis=0, keepdims=True)
                        top = jnp.maximum(top, best * C2 + bias[jj][i])
                    total = jnp.zeros((1, 128), F32)
                    part = jnp.zeros((1, 128), F32)
                    for i in range(4):
                        e = jnp.exp2(s[i * 128 : (i + 1) * 128, cols] * C2 - (top - bias[jj][i]))
                        total += jnp.sum(e, axis=0, keepdims=True)
                        part += jnp.sum(e * t[i * 128 : (i + 1) * 128, cols], axis=0, keepdims=True)
                    held[h, 0:1, out] = top
                    held[h, 1:2, out] = total
                    held[h, 2:3, out] = part

    store_rows(stat, held)


def video_stats_kernel(scal, vq, vg, ak, av, stat, held):
    half = scal[S_AUD]
    first_rows(held)
    for q in range(ROWS // CH):

        @pl.when(chunk_active(scal, half, q))
        def _():
            rows = slice(q * CH, (q + 1) * CH)
            bias = [[bias_of(scal, half, i, q * 4 + j) for j in range(4)] for i in range(4)]
            for h in range(NH):
                hc = head_cols(0, h)
                s = dot_nt(ak[rows, hc], vq[:, hc])
                t = dot_nt(av[rows, hc], vg[:, hc])
                for i in range(4):
                    cols = slice(i * 128, (i + 1) * 128)
                    old = held[h, 0:1, cols]
                    top = old
                    for j in range(4):
                        best = jnp.max(s[j * 64 : (j + 1) * 64, cols], axis=0, keepdims=True)
                        top = jnp.maximum(top, best * C2 + bias[i][j])
                    shrink = jnp.exp2(old - top)
                    total = held[h, 1:2, cols] * shrink
                    part = held[h, 2:3, cols] * shrink
                    for j in range(4):
                        e = jnp.exp2(s[j * 64 : (j + 1) * 64, cols] * C2 - (top - bias[i][j]))
                        total += jnp.sum(e, axis=0, keepdims=True)
                        part += jnp.sum(e * t[j * 64 : (j + 1) * 64, cols], axis=0, keepdims=True)
                    held[h, 0:1, cols] = top
                    held[h, 1:2, cols] = total
                    held[h, 2:3, cols] = part

    store_rows(stat, held)


def statistics(kernel, name, scal, *arrays):
    scratch = [pltpu.VMEM((NH, 8, ROWS), F32)]
    return call(kernel, 4, [STAT], scratch, 24, 2 * PAIRS, 3_200_000, name, scal, *arrays)[0]


def merge_kernel(final, scal, *refs):
    *ins, out = refs
    tops = [r[0] for r in ins]
    top = functools.reduce(jnp.maximum, tops)
    weights = [jnp.exp2(t - top) for t in tops]
    total = sum(r[1] * w for r, w in zip(ins, weights))
    part = sum(r[2] * w for r, w in zip(ins, weights))
    if final:
        out[0] = top + jnp.log(total) * math.log2(math.e)
        out[1] = part / total
    else:
        out[0] = top
        out[1] = total
        out[2] = part


def merge(scal, stats, final):
    kernel = functools.partial(merge_kernel, final)
    return call(kernel, len(stats), [BOTH if final else STAT], [], 4, 200_000, 200_000, "merge", scal, *stats)[0]


def video_queries(scal, half, q, h, ak, av, vq, vg, vstat, prob, dscore):
    s = dot_nt(ak, vq)
    t = dot_nt(av, vg)
    lses = vstat[0, pl.ds(h, 1), :]
    deltas = vstat[1, pl.ds(h, 1), :]
    for i in range(4):
        cols = slice(i * 128, (i + 1) * 128)
        lse, delta = lses[:, cols], deltas[:, cols]
        for j in range(4):
            rows = slice(j * 64, (j + 1) * 64)
            p = jnp.exp2(s[rows, cols] * C2 - (lse - bias_of(scal, half, i, q * 4 + j)))
            prob[rows, cols] = p.astype(BF16)
            dscore[rows, cols] = (p * (t[rows, cols] - delta) * SCALE).astype(BF16)


def audio_queries(scal, half, q, h, aq, ag, vk, vv, astat, prob, dscore):
    s = dot_nt(vk, aq)
    t = dot_nt(vv, ag)
    lses = astat[0, pl.ds(h, 1), :]
    deltas = astat[1, pl.ds(h, 1), :]
    for jj in range(CH // 128):
        cols = slice(jj * 128, (jj + 1) * 128)
        out = slice(q * CH + jj * 128, q * CH + jj * 128 + 128)
        lse, delta = lses[:, out], deltas[:, out]
        for i in range(4):
            rows = slice(i * 128, (i + 1) * 128)
            p = jnp.exp2(s[rows, cols] * C2 - (lse - pair_bias(scal, half, i, q * 4 + jj * 2)))
            prob[rows, cols] = p.astype(BF16)
            dscore[rows, cols] = (p * (t[rows, cols] - delta) * SCALE).astype(BF16)


def own_video_kernel(scal, vq, vg, ak, av, vstat, keep, send, dvq, prob, dscore, acc):
    half = scal[S_AUD]
    acc[...] = jnp.zeros_like(acc)
    for q in range(ROWS // CH):
        rows = slice(q * CH, (q + 1) * CH)
        active = chunk_active(scal, half, q)

        @pl.when(active)
        def _():
            for step, out in enumerate((keep, send)):
                g = lax.rem(scal[S_CORE] + step, 2)
                for r in range(HALF):
                    hc = head_cols(g, r)
                    at = step * HALF + r
                    video_queries(
                        scal, half, q, g * HALF + r, ak[rows, hc], av[rows, hc], vq[:, hc], vg[:, hc], vstat,
                        prob.at[at], dscore.at[at],
                    )
                    ds = dscore[at]
                    out[0, rows, r * DH : (r + 1) * DH] = dot_nn(ds, vq[:, hc]).astype(BF16)
                    out[1, rows, r * DH : (r + 1) * DH] = dot_nn(prob[at], vg[:, hc]).astype(BF16)
                    acc[at] += dot_nn(ak[rows, hc].T, ds)

        @pl.when(jnp.logical_not(active))
        def _():
            for out in (keep, send):
                for k in range(2):
                    out[k, rows, :] = jnp.zeros((CH, WIDE), BF16)

    for step in range(2):
        g = lax.rem(scal[S_CORE] + step, 2)
        for r in range(HALF):
            dvq[:, head_cols(g, r)] = acc[step * HALF + r].T


def own_audio_kernel(scal, vk, vv, aq, ag, astat, keep, send, dvk, dvv, prob, dscore):
    half = scal[S_AUD]
    dvk[...] = jnp.zeros_like(dvk)
    dvv[...] = jnp.zeros_like(dvv)
    for q in range(ROWS // CH):
        rows = slice(q * CH, (q + 1) * CH)
        active = chunk_active(scal, half, q)

        @pl.when(active)
        def _():
            for step, out in enumerate((keep, send)):
                g = lax.rem(scal[S_CORE] + step, 2)
                for r in range(HALF):
                    hc = head_cols(g, r)
                    at = step * HALF + r
                    audio_queries(
                        scal, half, q, g * HALF + r, aq[rows, hc], ag[rows, hc], vk[:, hc], vv[:, hc], astat,
                        prob.at[at], dscore.at[at],
                    )
                    ds = dscore[at]
                    out[0, rows, r * DH : (r + 1) * DH] = dot_nn(vk[:, hc].T, ds).T.astype(BF16)
                    dvk[:, hc] += dot_nn(ds, aq[rows, hc])
                    dvv[:, hc] += dot_nn(prob[at], ag[rows, hc])

        @pl.when(jnp.logical_not(active))
        def _():
            for out in (keep, send):
                out[0, rows, :] = jnp.zeros((CH, WIDE), BF16)


MINE = (ROWS, NH * DH)


def own_video(scal, vq, vg, ak, av, vstat):
    part = ((2, ROWS, WIDE), BF16)
    scratch = [pltpu.VMEM((NH, CH, ROWS), BF16)] * 2 + [pltpu.VMEM((NH, DH, ROWS), F32)]
    return call(
        own_video_kernel, 5, [part, part, (MINE, F32)], scratch, 28, 5 * PAIRS, 6_400_000, "own_video",
        scal, vq, vg, ak, av, vstat,
    )


def own_audio(scal, vk, vv, aq, ag, astat):
    part = ((1, ROWS, WIDE), BF16)
    scratch = [pltpu.VMEM((NH, ROWS, CH), BF16)] * 2
    return call(
        own_audio_kernel, 5, [part, part, (MINE, F32), (MINE, F32)], scratch, 28, 5 * PAIRS, 6_400_000, "own_audio",
        scal, vk, vv, aq, ag, astat,
    )


def collect(scal, pieces, audio, which):
    for d in range(4):
        y = lax.rem(scal[S_Y] + 4 - d, 4)
        for swapped in range(2):
            core = scal[S_CORE] if swapped == 0 else 1 - scal[S_CORE]
            for e in range(4):
                z = lax.rem(scal[S_Z] + 4 - e, 4)
                row = pl.multiple_of(y * 128 + z * 32 + core * 16, 16)
                for at, k in enumerate(which):
                    audio[at, pl.ds(row, 16), :] = pieces[2 * d + swapped][e, k]


def other_video_kernel(scal, vq, vg, vstat, pvq, *refs):
    pieces, (dvq, audio, prob, dscore, acc) = refs[:8], refs[8:]
    half = 1 - scal[S_AUD]
    collect(scal, pieces, audio, (1, 2))
    acc[...] = jnp.zeros_like(acc)
    for q in range(ROWS // CH):

        @pl.when(chunk_active(scal, half, q))
        def _():
            rows = slice(q * CH, (q + 1) * CH)
            for h in range(NH):
                hc = head_cols(0, h)
                ak, av = audio[0, rows, hc], audio[1, rows, hc]
                video_queries(scal, half, q, h, ak, av, vq[:, hc], vg[:, hc], vstat, prob.at[h], dscore.at[h])
                acc[h] += dot_nn(ak.T, dscore[h])

    for h in range(NH):
        hc = head_cols(0, h)
        dvq[:, hc] = (pvq[:, hc] + acc[h].T).astype(BF16)


def other_audio_kernel(scal, vk, vv, astat, pvk, pvv, *refs):
    pieces, (dvk, dvv, audio, prob, dscore, acck, accv) = refs[:8], refs[8:]
    half = 1 - scal[S_AUD]
    collect(scal, pieces, audio, (0, 3))
    acck[...] = pvk[...]
    accv[...] = pvv[...]
    for q in range(ROWS // CH):

        @pl.when(chunk_active(scal, half, q))
        def _():
            rows = slice(q * CH, (q + 1) * CH)
            for h in range(NH):
                hc = head_cols(0, h)
                aq, ag = audio[0, rows, hc], audio[1, rows, hc]
                audio_queries(scal, half, q, h, aq, ag, vk[:, hc], vv[:, hc], astat, prob.at[h], dscore.at[h])
                acck[:, hc] += dot_nn(dscore[h], aq)
                accv[:, hc] += dot_nn(prob[h], ag)

    dvk[...] = acck[...].astype(BF16)
    dvv[...] = accv[...].astype(BF16)


def other_video(scal, vq, vg, vstat, pvq, pieces):
    scratch = [pltpu.VMEM((2,) + MINE, BF16)] + [pltpu.VMEM((NH, CH, ROWS), BF16)] * 2
    scratch += [pltpu.VMEM((NH, DH, ROWS), F32)]
    return call(
        other_video_kernel, 12, [(MINE, BF16)], scratch, 28, 3 * PAIRS, 6_400_000, "other_video",
        scal, vq, vg, vstat, pvq, *pieces,
    )[0]


def other_audio(scal, vk, vv, astat, pvk, pvv, pieces):
    scratch = [pltpu.VMEM((2,) + MINE, BF16)] + [pltpu.VMEM((NH, ROWS, CH), BF16)] * 2
    scratch += [pltpu.VMEM(MINE, F32)] * 2
    return call(
        other_audio_kernel, 13, [(MINE, BF16), (MINE, BF16)], scratch, 28, 4 * PAIRS, 6_400_000, "other_audio",
        scal, vk, vv, astat, pvk, pvv, *pieces,
    )


def shift(x, axis, d):
    return lax.ppermute(x, axis, [(i, (i + d) % 4) for i in range(4)])


def swap(x, axis):
    return lax.ppermute(x, axis, [(0, 1), (1, 0)])


def take_kernel(scal, aq, ak, av, ag, out):
    for k, ref in enumerate((aq, ak, av, ag)):
        out[k] = ref[...]


def take_share(scal, *audio):
    def block(i, scal):
        return ((scal[S_Y] * 4 + scal[S_Z]) * 2 + scal[S_CORE], 0)

    return pl.pallas_call(
        take_kernel,
        grid_spec=pltpu.PrefetchScalarGridSpec(
            num_scalar_prefetch=1,
            grid=(1,),
            in_specs=[pl.BlockSpec((16, NH * DH), block)] * 4,
            out_specs=pl.BlockSpec((4, 16, NH * DH), lambda i, scal: (0, 0, 0)),
        ),
        out_shape=jax.ShapeDtypeStruct((4, 16, NH * DH), BF16),
        compiler_params=limit(8),
        cost_estimate=pl.CostEstimate(flops=0, bytes_accessed=200_000, transcendentals=0),
        name="take_share",
    )(scal, *audio)


def along(x, axis, held=None):
    return [x if held is None else after(x, held)] + [shift(x, axis, d) for d in (1, 2, 3)]


def both_cores(parts):
    return [p for part in parts for p in (part, swap(part, "core"))]


def after(x, *others):
    return lax.optimization_barrier((x, *others))[0]


def add_kernel(groups, axis, size, scal, *refs):
    outs = refs[sum(groups) :]
    at = 0
    first = 0
    for count in groups:
        ins = refs[at : at + count]
        n = ins[0].shape[0]
        for d, out in enumerate(outs):
            if size is None:
                rows = slice(None)
            else:
                rows = pl.ds(pl.multiple_of(lax.rem(scal[axis] + d, 4) * size, size), size)
            total = sum(r[:, rows, :].astype(F32) for r in ins)
            out[first : first + n] = total.astype(BF16)
        at += count
        first += n


def add_and_cut(scal, groups, axis):
    parts = [part for group in groups for part in group]
    n = sum(group[0].shape[0] for group in groups)
    _, rows, width = parts[0].shape
    size = None if axis is None else rows // 4
    outs = 1 if axis is None else 4
    shape = jax.ShapeDtypeStruct((n, rows if axis is None else size, width), BF16)
    return pl.pallas_call(
        functools.partial(add_kernel, [len(group) for group in groups], axis, size),
        in_specs=[pl.BlockSpec(memory_space=pltpu.SMEM)] + [pl.BlockSpec(memory_space=pltpu.VMEM)] * len(parts),
        out_specs=[pl.BlockSpec(memory_space=pltpu.VMEM)] * outs,
        out_shape=[shape] * outs,
        compiler_params=limit(8),
        cost_estimate=pl.CostEstimate(
            flops=n * rows * width, bytes_accessed=4 * n * rows * width, transcendentals=0
        ),
        name="add_and_cut",
    )(scal, *parts)


def place_kernel(n, scal, *refs):
    pieces, outs = refs[:8], refs[8:]
    for d in range(4):
        y = lax.rem(scal[S_Y] + 4 - d, 4)
        for swapped in range(2):
            core = scal[S_CORE] if swapped == 0 else 1 - scal[S_CORE]
            cols = pl.ds(pl.multiple_of(core * (HALF * DH), HALF * DH), HALF * DH)
            for e in range(4):
                z = lax.rem(scal[S_Z] + 4 - e, 4)
                row = pl.multiple_of(y * 128 + z * 32, 32)
                for k in range(n):
                    outs[k][pl.ds(row, 32), cols] = pieces[2 * d + swapped][e, k]


def place(scal, pieces):
    n = pieces[0].shape[1]
    shape = jax.ShapeDtypeStruct((ROWS, NH * DH), BF16)
    return pl.pallas_call(
        functools.partial(place_kernel, n),
        in_specs=[pl.BlockSpec(memory_space=pltpu.SMEM)] + [pl.BlockSpec(memory_space=pltpu.VMEM)] * 8,
        out_specs=[pl.BlockSpec(memory_space=pltpu.VMEM)] * n,
        out_shape=[shape] * n,
        compiler_params=limit(8),
        cost_estimate=pl.CostEstimate(flops=0, bytes_accessed=4 * n * ROWS * NH * DH, transcendentals=0),
        name="place",
    )(scal, *pieces)


def per_device(vq, vk, vv, vg, aq, ak, av, ag, alignment):
    y, z, core, aud = (lax.axis_index(name) for name in ("y", "z", "core", "aud"))
    vid = (y * 4 + z) * 2 + core
    mask = lax.dynamic_slice(alignment, (vid * 4, 0), (4, 16)).reshape(64)
    scal = jnp.concatenate([jnp.stack([y, z, core, aud]).astype(jnp.int32), mask])

    mine = take_share(scal, aq, ak, av, ag)
    share = swap(mine, "aud")
    apart = statistics(audio_stats_kernel, "audio_stats", after(scal, mine), vk, vv, aq, ag)
    share = after(share, apart)
    apart = merge(scal, [apart, swap(apart, "core")], False)
    vpart = statistics(video_stats_kernel, "video_stats", after(scal, apart, share), vq, vg, ak, av)
    apart = merge(scal, along(apart, "z", vpart), False)
    line = jnp.stack(along(share, "z", vpart))
    vstat = merge(scal, [vpart, swap(vpart, "aud")], True)
    keep_v, send_v, dvq = own_video(after(scal, apart, line), vq, vg, ak, av, vstat)
    astat = merge(scal, along(apart, "y", dvq), True)
    pieces = both_cores(along(line, "y", dvq))
    astat_other = swap(astat, "aud")
    keep_a, send_a, dvk, dvv = own_audio(scal, vk, vv, aq, ag, astat)
    pairs = [[after(keep_v, astat_other), swap(send_v, "core")], [keep_a, swap(send_a, "core")]]
    cut = add_and_cut(scal, pairs, S_Y)
    dvq = other_video(after(scal, cut[0]), vq, vg, vstat, dvq, pieces)
    cut = add_and_cut(scal, [[after(cut[0], dvq)] + [shift(cut[d], "y", d) for d in (1, 2, 3)]], S_Z)
    piece = add_and_cut(scal, [[cut[0]] + [shift(cut[d], "z", d) for d in (1, 2, 3)]], None)[0]
    line = jnp.stack(along(piece, "z"))
    dvk, dvv = other_audio(after(scal, line), vk, vv, astat_other, dvk, dvv, pieces)
    dak, dav, daq = place(scal, both_cores([after(part, dvk) for part in along(line, "y")]))
    return dvq, dvk, dvv, daq, dak, dav


def solution(mesh):
    grid = Mesh(mesh.devices.reshape(4, 4, 2, 2, 4), ("y", "z", "core", "aud", "head"))
    video = P(("y", "z", "core"), "head")
    audio = P("aud", "head")
    return jax.shard_map(
        per_device,
        mesh=grid,
        in_specs=(video,) * 4 + (audio,) * 4 + (P(),),
        out_specs=(video,) * 3 + (audio,) * 3,
        check_vma=False,
    )
```

```python
import functools
import math

import jax
import jax.numpy as jnp
from jax import lax
from jax.experimental import pallas as pl
from jax.experimental.pallas import tpu as pltpu
from jax.sharding import Mesh
from jax.sharding import PartitionSpec as P

DH = 128
VBLK = 128
ABLK = 64
NH = 6
HALF = 3
ROWS = 512
CH = 256
SHARE = 64
SCALE = DH ** -0.5
C2 = SCALE * math.log2(math.e)
MASKED = -1e30
FLOOR = -1e29
WIDE = HALF * DH
F32 = jnp.float32
BF16 = jnp.bfloat16
STAT = ((3, 8, ROWS), F32)
BOTH = ((2, 8, ROWS), F32)

S_Y, S_Z, S_CORE, S_AUD, S_MASK = 0, 1, 2, 3, 4

MIB = 1024 * 1024


def cost(us):
    return pl.CostEstimate(flops=us * 1_000_000_000, bytes_accessed=100_000, transcendentals=0)


def limit(mib):
    return pltpu.CompilerParams(vmem_limit_bytes=mib * MIB)


def call(kernel, ins, outs, scratch, mib, us, name, scal, *arrays):
    vmem = pl.BlockSpec(memory_space=pltpu.VMEM)
    return pl.pallas_call(
        kernel,
        in_specs=[pl.BlockSpec(memory_space=pltpu.SMEM)] + [vmem] * ins,
        out_specs=[vmem] * len(outs),
        out_shape=[jax.ShapeDtypeStruct(shape, dtype) for shape, dtype in outs],
        scratch_shapes=scratch,
        compiler_params=limit(mib),
        cost_estimate=cost(us),
        name=name,
    )(scal, *arrays)


def dot_nt(a, b):
    return lax.dot_general(a, b, (((1,), (1,)), ((), ())), preferred_element_type=F32)


def dot_nn(a, b):
    return lax.dot_general(a, b, (((1,), (0,)), ((), ())), preferred_element_type=F32)


def bias_of(scal, half, i, j):
    return jnp.where(scal[S_MASK + i * 16 + half * 8 + j] > 0, 0.0, MASKED)


def chunk_active(scal, half, q):
    c = scal[S_Y] * 4 + scal[S_Z]
    first = half * 8 + q * (CH // ABLK)
    return jnp.logical_and(first <= c + 3, first + CH // ABLK - 1 >= c - 3)


def pair_bias(scal, half, i, j):
    lane = lax.broadcasted_iota(jnp.int32, (1, 128), 1)
    return jnp.where(lane < ABLK, bias_of(scal, half, i, j), bias_of(scal, half, i, j + 1))


def head_cols(g, r):
    if isinstance(g, int):
        return slice(g * WIDE + r * DH, g * WIDE + (r + 1) * DH)
    return pl.ds(pl.multiple_of(g * WIDE + r * DH, DH), DH)


def first_rows(held):
    for h in range(NH):
        held[h, 0:1, :] = jnp.full((1, ROWS), FLOOR, F32)
        held[h, 1:2, :] = jnp.zeros((1, ROWS), F32)
        held[h, 2:3, :] = jnp.zeros((1, ROWS), F32)


def store_rows(stat, held):
    for k in range(3):
        for h in range(NH):
            stat[k, h : h + 1, :] = held[h, k : k + 1, :]
        stat[k, NH:8, :] = jnp.ones((8 - NH, ROWS), F32)


def shared_rows(scal):
    return pl.ds(pl.multiple_of(scal[S_Y] * 128 + scal[S_CORE] * SHARE, SHARE), SHARE)


def audio_stats_kernel(scal, vk, vv, aq, ag, stat, share, held):
    half = scal[S_AUD]
    first_rows(held)
    for q in range(ROWS // CH):

        @pl.when(chunk_active(scal, half, q))
        def _():
            rows = slice(q * CH, (q + 1) * CH)
            bias = [[pair_bias(scal, half, i, q * 4 + jj * 2) for i in range(4)] for jj in range(2)]
            for h in range(NH):
                hc = head_cols(0, h)
                s = dot_nt(vk[:, hc], aq[rows, hc])
                t = dot_nt(vv[:, hc], ag[rows, hc])
                for jj in range(CH // 128):
                    cols = slice(jj * 128, (jj + 1) * 128)
                    out = slice(q * CH + jj * 128, q * CH + jj * 128 + 128)
                    top = jnp.full((1, 128), FLOOR, F32)
                    for i in range(4):
                        best = jnp.max(s[i * 128 : (i + 1) * 128, cols], axis=0, keepdims=True)
                        top = jnp.maximum(top, best * C2 + bias[jj][i])
                    total = jnp.zeros((1, 128), F32)
                    part = jnp.zeros((1, 128), F32)
                    for i in range(4):
                        e = jnp.exp2(s[i * 128 : (i + 1) * 128, cols] * C2 - (top - bias[jj][i]))
                        total += jnp.sum(e, axis=0, keepdims=True)
                        part += jnp.sum(e * t[i * 128 : (i + 1) * 128, cols], axis=0, keepdims=True)
                    held[h, 0:1, out] = top
                    held[h, 1:2, out] = total
                    held[h, 2:3, out] = part

    store_rows(stat, held)
    rows = shared_rows(scal)
    share[0] = aq[rows, :]
    share[1] = ag[rows, :]


def video_stats_kernel(scal, vq, vg, ak, av, audio_share, stat, share, held):
    half = scal[S_AUD]
    first_rows(held)
    for q in range(ROWS // CH):

        @pl.when(chunk_active(scal, half, q))
        def _():
            rows = slice(q * CH, (q + 1) * CH)
            bias = [[bias_of(scal, half, i, q * 4 + j) for j in range(4)] for i in range(4)]
            for h in range(NH):
                hc = head_cols(0, h)
                s = dot_nt(ak[rows, hc], vq[:, hc])
                t = dot_nt(av[rows, hc], vg[:, hc])
                for i in range(4):
                    cols = slice(i * 128, (i + 1) * 128)
                    old = held[h, 0:1, cols]
                    top = old
                    for j in range(4):
                        best = jnp.max(s[j * 64 : (j + 1) * 64, cols], axis=0, keepdims=True)
                        top = jnp.maximum(top, best * C2 + bias[i][j])
                    shrink = jnp.exp2(old - top)
                    total = held[h, 1:2, cols] * shrink
                    part = held[h, 2:3, cols] * shrink
                    for j in range(4):
                        e = jnp.exp2(s[j * 64 : (j + 1) * 64, cols] * C2 - (top - bias[i][j]))
                        total += jnp.sum(e, axis=0, keepdims=True)
                        part += jnp.sum(e * t[j * 64 : (j + 1) * 64, cols], axis=0, keepdims=True)
                    held[h, 0:1, cols] = top
                    held[h, 1:2, cols] = total
                    held[h, 2:3, cols] = part

    store_rows(stat, held)
    rows = shared_rows(scal)
    share[0] = audio_share[0]
    share[1] = ak[rows, :]
    share[2] = av[rows, :]
    share[3] = audio_share[1]


def statistics(kernel, name, shared, scal, *arrays):
    scratch = [pltpu.VMEM((NH, 8, ROWS), F32)]
    share = ((shared, SHARE, NH * DH), BF16)
    return call(kernel, len(arrays), [STAT, share], scratch, 24, 20, name, scal, *arrays)


def merge_kernel(final, scal, *refs):
    *ins, out = refs
    tops = [r[0] for r in ins]
    top = functools.reduce(jnp.maximum, tops)
    weights = [jnp.exp2(t - top) for t in tops]
    total = sum(r[1] * w for r, w in zip(ins, weights))
    part = sum(r[2] * w for r, w in zip(ins, weights))
    if final:
        out[0] = top + jnp.log(total) * math.log2(math.e)
        out[1] = part / total
    else:
        out[0] = top
        out[1] = total
        out[2] = part


def merge(scal, stats, final):
    kernel = functools.partial(merge_kernel, final)
    return call(kernel, len(stats), [BOTH if final else STAT], [], 4, 1, "merge", scal, *stats)[0]


def video_queries(scal, half, q, h, ak, av, vq, vg, vstat, prob, dscore):
    s = dot_nt(ak, vq)
    t = dot_nt(av, vg)
    lses = vstat[0, pl.ds(h, 1), :]
    deltas = vstat[1, pl.ds(h, 1), :]
    for i in range(4):
        cols = slice(i * 128, (i + 1) * 128)
        lse, delta = lses[:, cols], deltas[:, cols]
        for j in range(4):
            rows = slice(j * 64, (j + 1) * 64)
            p = jnp.exp2(s[rows, cols] * C2 - (lse - bias_of(scal, half, i, q * 4 + j)))
            prob[rows, cols] = p.astype(BF16)
            dscore[rows, cols] = (p * (t[rows, cols] - delta) * SCALE).astype(BF16)


def audio_queries(scal, half, q, h, aq, ag, vk, vv, astat, prob, dscore):
    s = dot_nt(vk, aq)
    t = dot_nt(vv, ag)
    lses = astat[0, pl.ds(h, 1), :]
    deltas = astat[1, pl.ds(h, 1), :]
    for jj in range(CH // 128):
        cols = slice(jj * 128, (jj + 1) * 128)
        out = slice(q * CH + jj * 128, q * CH + jj * 128 + 128)
        lse, delta = lses[:, out], deltas[:, out]
        for i in range(4):
            rows = slice(i * 128, (i + 1) * 128)
            p = jnp.exp2(s[rows, cols] * C2 - (lse - pair_bias(scal, half, i, q * 4 + jj * 2)))
            prob[rows, cols] = p.astype(BF16)
            dscore[rows, cols] = (p * (t[rows, cols] - delta) * SCALE).astype(BF16)


def own_video_kernel(scal, vq, vg, ak, av, vstat, keep, send, dvq, prob, dscore, acc):
    half = scal[S_AUD]
    acc[...] = jnp.zeros_like(acc)
    for q in range(ROWS // CH):
        rows = slice(q * CH, (q + 1) * CH)
        active = chunk_active(scal, half, q)

        @pl.when(active)
        def _():
            for step, out in enumerate((keep, send)):
                g = lax.rem(scal[S_CORE] + step, 2)
                for r in range(HALF):
                    hc = head_cols(g, r)
                    at = step * HALF + r
                    video_queries(
                        scal, half, q, g * HALF + r, ak[rows, hc], av[rows, hc], vq[:, hc], vg[:, hc], vstat,
                        prob.at[at], dscore.at[at],
                    )
                    ds = dscore[at]
                    out[0, rows, r * DH : (r + 1) * DH] = dot_nn(ds, vq[:, hc]).astype(BF16)
                    out[1, rows, r * DH : (r + 1) * DH] = dot_nn(prob[at], vg[:, hc]).astype(BF16)
                    acc[at] += dot_nn(ak[rows, hc].T, ds)

        @pl.when(jnp.logical_not(active))
        def _():
            for out in (keep, send):
                for k in range(2):
                    out[k, rows, :] = jnp.zeros((CH, WIDE), BF16)

    for step in range(2):
        g = lax.rem(scal[S_CORE] + step, 2)
        for r in range(HALF):
            dvq[:, head_cols(g, r)] = acc[step * HALF + r].T


def own_audio_kernel(scal, vk, vv, aq, ag, astat, keep, send, dvk, dvv, prob, dscore):
    half = scal[S_AUD]
    dvk[...] = jnp.zeros_like(dvk)
    dvv[...] = jnp.zeros_like(dvv)
    for q in range(ROWS // CH):
        rows = slice(q * CH, (q + 1) * CH)
        active = chunk_active(scal, half, q)

        @pl.when(active)
        def _():
            for step, out in enumerate((keep, send)):
                g = lax.rem(scal[S_CORE] + step, 2)
                for r in range(HALF):
                    hc = head_cols(g, r)
                    at = step * HALF + r
                    audio_queries(
                        scal, half, q, g * HALF + r, aq[rows, hc], ag[rows, hc], vk[:, hc], vv[:, hc], astat,
                        prob.at[at], dscore.at[at],
                    )
                    ds = dscore[at]
                    out[0, rows, r * DH : (r + 1) * DH] = dot_nn(vk[:, hc].T, ds).T.astype(BF16)
                    dvk[:, hc] += dot_nn(ds, aq[rows, hc])
                    dvv[:, hc] += dot_nn(prob[at], ag[rows, hc])

        @pl.when(jnp.logical_not(active))
        def _():
            for out in (keep, send):
                out[0, rows, :] = jnp.zeros((CH, WIDE), BF16)


MINE = (ROWS, NH * DH)


def own_video(scal, vq, vg, ak, av, vstat):
    part = ((2, ROWS, WIDE), BF16)
    scratch = [pltpu.VMEM((NH, CH, ROWS), BF16)] * 2 + [pltpu.VMEM((NH, DH, ROWS), F32)]
    return call(
        own_video_kernel, 5, [part, part, (MINE, F32)], scratch, 28, 20, "own_video",
        scal, vq, vg, ak, av, vstat,
    )


def own_audio(scal, vk, vv, aq, ag, astat):
    part = ((1, ROWS, WIDE), BF16)
    scratch = [pltpu.VMEM((NH, ROWS, CH), BF16)] * 2
    return call(
        own_audio_kernel, 5, [part, part, (MINE, F32), (MINE, F32)], scratch, 28, 20, "own_audio",
        scal, vk, vv, aq, ag, astat,
    )


def collect(scal, pieces, audio, which):
    for d in range(4):
        y = lax.rem(scal[S_Y] + 4 - d, 4)
        for swapped in range(2):
            core = scal[S_CORE] if swapped == 0 else 1 - scal[S_CORE]
            row = pl.multiple_of(y * 128 + core * SHARE, SHARE)
            for at, k in enumerate(which):
                audio[at, pl.ds(row, SHARE), :] = pieces[2 * d + swapped][k]


def other_video_kernel(scal, vq, vg, vstat, pvq, *refs):
    pieces, (dvq, audio, prob, dscore, acc) = refs[:8], refs[8:]
    half = 1 - scal[S_AUD]
    collect(scal, pieces, audio, (1, 2))
    acc[...] = jnp.zeros_like(acc)
    for q in range(ROWS // CH):

        @pl.when(chunk_active(scal, half, q))
        def _():
            rows = slice(q * CH, (q + 1) * CH)
            for h in range(NH):
                hc = head_cols(0, h)
                ak, av = audio[0, rows, hc], audio[1, rows, hc]
                video_queries(scal, half, q, h, ak, av, vq[:, hc], vg[:, hc], vstat, prob.at[h], dscore.at[h])
                acc[h] += dot_nn(ak.T, dscore[h])

    for h in range(NH):
        hc = head_cols(0, h)
        dvq[:, hc] = (pvq[:, hc] + acc[h].T).astype(BF16)


def other_audio_kernel(scal, vk, vv, astat, pvk, pvv, *refs):
    pieces, (dvk, dvv, audio, prob, dscore, acck, accv) = refs[:8], refs[8:]
    half = 1 - scal[S_AUD]
    collect(scal, pieces, audio, (0, 3))
    acck[...] = pvk[...]
    accv[...] = pvv[...]
    for q in range(ROWS // CH):

        @pl.when(chunk_active(scal, half, q))
        def _():
            rows = slice(q * CH, (q + 1) * CH)
            for h in range(NH):
                hc = head_cols(0, h)
                aq, ag = audio[0, rows, hc], audio[1, rows, hc]
                audio_queries(scal, half, q, h, aq, ag, vk[:, hc], vv[:, hc], astat, prob.at[h], dscore.at[h])
                acck[:, hc] += dot_nn(dscore[h], aq)
                accv[:, hc] += dot_nn(prob[h], ag)

    dvk[...] = acck[...].astype(BF16)
    dvv[...] = accv[...].astype(BF16)


def other_video(scal, vq, vg, vstat, pvq, pieces):
    scratch = [pltpu.VMEM((2,) + MINE, BF16)] + [pltpu.VMEM((NH, CH, ROWS), BF16)] * 2
    scratch += [pltpu.VMEM((NH, DH, ROWS), F32)]
    return call(
        other_video_kernel, 12, [(MINE, BF16)], scratch, 28, 20, "other_video",
        scal, vq, vg, vstat, pvq, *pieces,
    )[0]


def other_audio(scal, vk, vv, astat, pvk, pvv, pieces):
    scratch = [pltpu.VMEM((2,) + MINE, BF16)] + [pltpu.VMEM((NH, ROWS, CH), BF16)] * 2
    scratch += [pltpu.VMEM(MINE, F32)] * 2
    return call(
        other_audio_kernel, 13, [(MINE, BF16), (MINE, BF16)], scratch, 28, 20, "other_audio",
        scal, vk, vv, astat, pvk, pvv, *pieces,
    )


def shift(x, axis, d):
    return lax.ppermute(x, axis, [(i, (i + d) % 4) for i in range(4)])


def swap(x, axis):
    return lax.ppermute(x, axis, [(0, 1), (1, 0)])


def along(x, axis, held=None):
    return [x if held is None else after(x, held)] + [shift(x, axis, d) for d in (1, 2, 3)]


def shards(cut, axis):
    return [cut[0]] + [shift(cut[d], axis, d) for d in (1, 2, 3)]


def both_cores(parts):
    return [p for part in parts for p in (part, swap(part, "core"))]


def after(x, *others):
    return lax.optimization_barrier((x, *others))[0]


def add_kernel(groups, axis, size, scal, *refs):
    outs = refs[sum(groups) :]
    at = 0
    first = 0
    for count in groups:
        ins = refs[at : at + count]
        n = ins[0].shape[0]
        for d, out in enumerate(outs):
            if size is None:
                rows = slice(None)
            else:
                rows = pl.ds(pl.multiple_of(lax.rem(scal[axis] + d, 4) * size, size), size)
            total = sum(r[:, rows, :].astype(F32) for r in ins)
            out[first : first + n] = total.astype(BF16)
        at += count
        first += n


def add_and_cut(scal, groups, axis):
    parts = [part for group in groups for part in group]
    n = sum(group[0].shape[0] for group in groups)
    _, rows, width = parts[0].shape
    size = None if axis is None else rows // 4
    outs = 1 if axis is None else 4
    shape = jax.ShapeDtypeStruct((n, rows if axis is None else size, width), BF16)
    return pl.pallas_call(
        functools.partial(add_kernel, [len(group) for group in groups], axis, size),
        in_specs=[pl.BlockSpec(memory_space=pltpu.SMEM)] + [pl.BlockSpec(memory_space=pltpu.VMEM)] * len(parts),
        out_specs=[pl.BlockSpec(memory_space=pltpu.VMEM)] * outs,
        out_shape=[shape] * outs,
        compiler_params=limit(8),
        cost_estimate=cost(1),
        name="add_and_cut",
    )(scal, *parts)


def place_kernel(n, scal, *refs):
    pieces, outs = refs[:8], refs[8:]
    for d in range(4):
        y = lax.rem(scal[S_Y] + 4 - d, 4)
        for swapped in range(2):
            core = scal[S_CORE] if swapped == 0 else 1 - scal[S_CORE]
            cols = pl.ds(pl.multiple_of(core * (HALF * DH), HALF * DH), HALF * DH)
            for e in range(4):
                z = lax.rem(scal[S_Z] + 4 - e, 4)
                row = pl.multiple_of(y * 128 + z * 32, 32)
                for k in range(n):
                    outs[k][pl.ds(row, 32), cols] = pieces[2 * d + swapped][e, k]


def place(scal, pieces):
    n = pieces[0].shape[1]
    shape = jax.ShapeDtypeStruct((ROWS, NH * DH), BF16)
    return pl.pallas_call(
        functools.partial(place_kernel, n),
        in_specs=[pl.BlockSpec(memory_space=pltpu.SMEM)] + [pl.BlockSpec(memory_space=pltpu.VMEM)] * 8,
        out_specs=[pl.BlockSpec(memory_space=pltpu.VMEM)] * n,
        out_shape=[shape] * n,
        compiler_params=limit(8),
        cost_estimate=cost(1),
        name="place",
    )(scal, *pieces)


def per_device(vq, vk, vv, vg, aq, ak, av, ag, alignment):
    y, z, core, aud = (lax.axis_index(name) for name in ("y", "z", "core", "aud"))
    vid = (y * 4 + z) * 2 + core
    mask = lax.dynamic_slice(alignment, (vid * 4, 0), (4, 16)).reshape(64)
    scal = jnp.concatenate([jnp.stack([y, z, core, aud]).astype(jnp.int32), mask])

    apart, share = statistics(audio_stats_kernel, "audio_stats", 2, scal, vk, vv, aq, ag)
    vpart, share = statistics(video_stats_kernel, "video_stats", 4, after(scal, apart), vq, vg, ak, av, share)
    apart = merge(scal, [after(apart, vpart), swap(apart, "core")], False)
    apart = merge(scal, along(apart, "z"), False)
    vstat = merge(scal, [vpart, swap(vpart, "aud")], True)
    keep_v, send_v, dvq = own_video(after(scal, apart), vq, vg, ak, av, vstat)
    astat = merge(scal, along(apart, "y", dvq), True)
    share = swap(after(share, astat), "aud")
    keep_a, send_a, dvk, dvv = own_audio(scal, vk, vv, aq, ag, astat)
    share = after(share, dvk)
    cut = add_and_cut(scal, [[keep_v, swap(send_v, "core")], [keep_a, swap(send_a, "core")]], S_Y)
    astat_other = swap(after(astat, cut[0]), "aud")
    cut = add_and_cut(scal, [shards(cut, "y")], S_Z)
    share = after(share, cut[0])
    own, first, third = share, shift(share, "y", 1), shift(share, "y", 3)
    shards_z = shards(cut, "z")
    piece = add_and_cut(scal, [[after(shards_z[0], astat_other)] + shards_z[1:]], None)[0]
    second = shift(after(share, piece), "y", 2)
    line = jnp.stack(along(after(piece, first, third), "z"))
    pieces = both_cores([own, first, after(second, line), third])
    dvq = other_video(after(scal, line), vq, vg, vstat, dvq, pieces)
    dvk, dvv = other_audio(after(scal, dvq), vk, vv, astat_other, dvk, dvv, pieces)
    gathered = along(line, "y")
    gathered = both_cores(gathered[:1]) + both_cores([after(part, dvk) for part in gathered[1:]])
    dak, dav, daq = place(scal, gathered)
    return dvq, dvk, dvv, daq, dak, dav


def solution(mesh):
    grid = Mesh(mesh.devices.reshape(4, 4, 2, 2, 4), ("y", "z", "core", "aud", "head"))
    video = P(("y", "z", "core"), "head")
    audio = P("aud", "head")
    return jax.shard_map(
        per_device,
        mesh=grid,
        in_specs=(video,) * 4 + (audio,) * 4 + (P(),),
        out_specs=(video,) * 3 + (audio,) * 3,
        check_vma=False,
    )
```

```python
import functools
import math

import jax
import jax.numpy as jnp
from jax import lax
from jax.experimental import pallas as pl
from jax.experimental.pallas import tpu as pltpu
from jax.sharding import Mesh
from jax.sharding import PartitionSpec as P

DH = 128
VBLK = 128
ABLK = 64
NH = 6
HALF = 3
ROWS = 512
CH = 256
SHARE = 64
SCALE = DH ** -0.5
C2 = SCALE * math.log2(math.e)
MASKED = -1e30
FLOOR = -1e29
WIDE = HALF * DH
F32 = jnp.float32
BF16 = jnp.bfloat16
STAT = ((3, 8, ROWS), F32)
BOTH = ((2, 8, ROWS), F32)

S_Y, S_Z, S_CORE, S_AUD, S_MASK = 0, 1, 2, 3, 4

MIB = 1024 * 1024


def cost(us):
    return pl.CostEstimate(flops=us * 1_000_000_000, bytes_accessed=100_000, transcendentals=0)


def limit(mib):
    return pltpu.CompilerParams(vmem_limit_bytes=mib * MIB)


def call(kernel, ins, outs, scratch, mib, us, name, scal, *arrays):
    vmem = pl.BlockSpec(memory_space=pltpu.VMEM)
    return pl.pallas_call(
        kernel,
        in_specs=[pl.BlockSpec(memory_space=pltpu.SMEM)] + [vmem] * ins,
        out_specs=[vmem] * len(outs),
        out_shape=[jax.ShapeDtypeStruct(shape, dtype) for shape, dtype in outs],
        scratch_shapes=scratch,
        compiler_params=limit(mib),
        cost_estimate=cost(us),
        name=name,
    )(scal, *arrays)


def dot_nt(a, b):
    return lax.dot_general(a, b, (((1,), (1,)), ((), ())), preferred_element_type=F32)


def dot_nn(a, b):
    return lax.dot_general(a, b, (((1,), (0,)), ((), ())), preferred_element_type=F32)


def bias_of(scal, half, i, j):
    return jnp.where(scal[S_MASK + i * 16 + half * 8 + j] > 0, 0.0, MASKED)


def chunk_active(scal, half, q):
    c = scal[S_Y] * 4 + scal[S_Z]
    first = half * 8 + q * (CH // ABLK)
    return jnp.logical_and(first <= c + 3, first + CH // ABLK - 1 >= c - 3)


def each_chunk(scal, half, body, idle=None):
    @pl.loop(0, ROWS // CH)
    def _(q):
        rows = pl.ds(pl.multiple_of(q * CH, CH), CH)
        active = chunk_active(scal, half, q)

        @pl.when(active)
        def _():
            body(q, rows)

        if idle is not None:

            @pl.when(jnp.logical_not(active))
            def _():
                idle(rows)


def each_head(body, together):
    @pl.loop(0, NH // together)
    def _(p):
        for u in range(together):
            body(together * p + u, u)


def pair_bias(scal, half, i, j):
    lane = lax.broadcasted_iota(jnp.int32, (1, 128), 1)
    return jnp.where(lane < ABLK, bias_of(scal, half, i, j), bias_of(scal, half, i, j + 1))


def head_cols(g, r):
    return pl.ds(pl.multiple_of(g * WIDE + r * DH, DH), DH)


def first_rows(held):
    for h in range(NH):
        held[h, 0:1, :] = jnp.full((1, ROWS), FLOOR, F32)
        held[h, 1:2, :] = jnp.zeros((1, ROWS), F32)
        held[h, 2:3, :] = jnp.zeros((1, ROWS), F32)


def store_rows(stat, held):
    for k in range(3):
        for h in range(NH):
            stat[k, h : h + 1, :] = held[h, k : k + 1, :]
        stat[k, NH:8, :] = jnp.ones((8 - NH, ROWS), F32)


def shared_rows(scal):
    return pl.ds(pl.multiple_of(scal[S_Y] * 128 + scal[S_CORE] * SHARE, SHARE), SHARE)


def audio_stats_kernel(scal, vk, vv, aq, ag, stat, share, held):
    half = scal[S_AUD]
    first_rows(held)

    def chunk(q, rows):
        bias = [[pair_bias(scal, half, i, q * 4 + jj * 2) for i in range(4)] for jj in range(2)]

        def head(h, u):
            hc = head_cols(0, h)
            s = dot_nt(vk[:, hc], aq[rows, hc])
            t = dot_nt(vv[:, hc], ag[rows, hc])
            for jj in range(CH // 128):
                cols = slice(jj * 128, (jj + 1) * 128)
                out = pl.ds(pl.multiple_of(q * CH + jj * 128, 128), 128)
                top = jnp.full((1, 128), FLOOR, F32)
                for i in range(4):
                    best = jnp.max(s[i * 128 : (i + 1) * 128, cols], axis=0, keepdims=True)
                    top = jnp.maximum(top, best * C2 + bias[jj][i])
                total = jnp.zeros((1, 128), F32)
                part = jnp.zeros((1, 128), F32)
                for i in range(4):
                    e = jnp.exp2(s[i * 128 : (i + 1) * 128, cols] * C2 - (top - bias[jj][i]))
                    total += jnp.sum(e, axis=0, keepdims=True)
                    part += jnp.sum(e * t[i * 128 : (i + 1) * 128, cols], axis=0, keepdims=True)
                held[h, 0:1, out] = top
                held[h, 1:2, out] = total
                held[h, 2:3, out] = part

        each_head(head, 3)

    each_chunk(scal, half, chunk)
    store_rows(stat, held)
    rows = shared_rows(scal)
    share[0] = aq[rows, :]
    share[1] = ag[rows, :]


def video_stats_kernel(scal, vq, vg, ak, av, audio_share, stat, share, held):
    half = scal[S_AUD]
    first_rows(held)

    def chunk(q, rows):
        bias = [[bias_of(scal, half, i, q * 4 + j) for j in range(4)] for i in range(4)]

        def head(h, u):
            hc = head_cols(0, h)
            s = dot_nt(ak[rows, hc], vq[:, hc])
            t = dot_nt(av[rows, hc], vg[:, hc])
            for i in range(4):
                cols = slice(i * 128, (i + 1) * 128)
                old = held[h, 0:1, cols]
                top = old
                for j in range(4):
                    best = jnp.max(s[j * 64 : (j + 1) * 64, cols], axis=0, keepdims=True)
                    top = jnp.maximum(top, best * C2 + bias[i][j])
                shrink = jnp.exp2(old - top)
                total = held[h, 1:2, cols] * shrink
                part = held[h, 2:3, cols] * shrink
                for j in range(4):
                    e = jnp.exp2(s[j * 64 : (j + 1) * 64, cols] * C2 - (top - bias[i][j]))
                    total += jnp.sum(e, axis=0, keepdims=True)
                    part += jnp.sum(e * t[j * 64 : (j + 1) * 64, cols], axis=0, keepdims=True)
                held[h, 0:1, cols] = top
                held[h, 1:2, cols] = total
                held[h, 2:3, cols] = part

        each_head(head, 3)

    each_chunk(scal, half, chunk)
    store_rows(stat, held)
    rows = shared_rows(scal)
    share[0] = audio_share[0]
    share[1] = ak[rows, :]
    share[2] = av[rows, :]
    share[3] = audio_share[1]


def statistics(kernel, name, shared, scal, *arrays):
    scratch = [pltpu.VMEM((NH, 8, ROWS), F32)]
    share = ((shared, SHARE, NH * DH), BF16)
    return call(kernel, len(arrays), [STAT, share], scratch, 24, 20, name, scal, *arrays)


def merge_kernel(final, scal, *refs):
    *ins, out = refs
    tops = [r[0] for r in ins]
    top = functools.reduce(jnp.maximum, tops)
    weights = [jnp.exp2(t - top) for t in tops]
    total = sum(r[1] * w for r, w in zip(ins, weights))
    part = sum(r[2] * w for r, w in zip(ins, weights))
    if final:
        out[0] = top + jnp.log(total) * math.log2(math.e)
        out[1] = part / total
    else:
        out[0] = top
        out[1] = total
        out[2] = part


def merge(scal, stats, final):
    kernel = functools.partial(merge_kernel, final)
    return call(kernel, len(stats), [BOTH if final else STAT], [], 4, 1, "merge", scal, *stats)[0]


def video_queries(scal, half, q, h, ak, av, vq, vg, vstat, prob, dscore):
    s = dot_nt(ak, vq)
    t = dot_nt(av, vg)
    lses = vstat[0, pl.ds(h, 1), :]
    deltas = vstat[1, pl.ds(h, 1), :]
    for i in range(4):
        cols = slice(i * 128, (i + 1) * 128)
        lse, delta = lses[:, cols], deltas[:, cols]
        for j in range(4):
            rows = slice(j * 64, (j + 1) * 64)
            p = jnp.exp2(s[rows, cols] * C2 - (lse - bias_of(scal, half, i, q * 4 + j)))
            prob[rows, cols] = p.astype(BF16)
            dscore[rows, cols] = (p * (t[rows, cols] - delta) * SCALE).astype(BF16)


def audio_queries(scal, half, q, h, aq, ag, vk, vv, astat, prob, dscore):
    s = dot_nt(vk, aq)
    t = dot_nt(vv, ag)
    lses = astat[0, pl.ds(h, 1), :]
    deltas = astat[1, pl.ds(h, 1), :]
    for jj in range(CH // 128):
        cols = slice(jj * 128, (jj + 1) * 128)
        first, second = slice(jj * 128, jj * 128 + 128), slice(CH + jj * 128, CH + jj * 128 + 128)
        lse = jnp.where(q == 0, lses[:, first], lses[:, second])
        delta = jnp.where(q == 0, deltas[:, first], deltas[:, second])
        for i in range(4):
            rows = slice(i * 128, (i + 1) * 128)
            p = jnp.exp2(s[rows, cols] * C2 - (lse - pair_bias(scal, half, i, q * 4 + jj * 2)))
            prob[rows, cols] = p.astype(BF16)
            dscore[rows, cols] = (p * (t[rows, cols] - delta) * SCALE).astype(BF16)


def own_head(scal, at):
    h = lax.rem(scal[S_CORE] * HALF + at, NH)
    return h, head_cols(0, h), at // HALF, head_cols(0, lax.rem(at, HALF))


def own_video_kernel(scal, vq, vg, ak, av, vstat, keep, send, dvq, prob, dscore, acc, sums):
    half = scal[S_AUD]
    acc[...] = jnp.zeros_like(acc)

    def chunk(q, rows):
        def head(at, u):
            h, hc, step, sc = own_head(scal, at)
            video_queries(
                scal, half, q, h, ak[rows, hc], av[rows, hc], vq[:, hc], vg[:, hc], vstat, prob.at[u], dscore.at[u]
            )
            ds = dscore[u]
            sums[step, 0, rows, sc] = dot_nn(ds, vq[:, hc]).astype(BF16)
            sums[step, 1, rows, sc] = dot_nn(prob[u], vg[:, hc]).astype(BF16)
            acc[at] += dot_nn(ak[rows, hc].T, ds)

        each_head(head, 3)

    def idle(rows):
        for step in range(2):
            for k in range(2):
                sums[step, k, rows, :] = jnp.zeros((CH, WIDE), BF16)

    each_chunk(scal, half, chunk, idle)
    keep[...] = sums[0]
    send[...] = sums[1]

    @pl.loop(0, NH)
    def _(at):
        dvq[:, own_head(scal, at)[1]] = acc[at].T


def own_audio_kernel(scal, vk, vv, aq, ag, astat, keep, send, dvk, dvv, prob, dscore, sums):
    half = scal[S_AUD]
    dvk[...] = jnp.zeros_like(dvk)
    dvv[...] = jnp.zeros_like(dvv)

    def chunk(q, rows):
        def head(at, u):
            h, hc, step, sc = own_head(scal, at)
            audio_queries(
                scal, half, q, h, aq[rows, hc], ag[rows, hc], vk[:, hc], vv[:, hc], astat, prob.at[u], dscore.at[u]
            )
            ds = dscore[u]
            sums[step, 0, rows, sc] = dot_nn(vk[:, hc].T, ds).T.astype(BF16)
            dvk[:, hc] += dot_nn(ds, aq[rows, hc])
            dvv[:, hc] += dot_nn(prob[u], ag[rows, hc])

        each_head(head, 3)

    def idle(rows):
        for step in range(2):
            sums[step, 0, rows, :] = jnp.zeros((CH, WIDE), BF16)

    each_chunk(scal, half, chunk, idle)
    keep[...] = sums[0]
    send[...] = sums[1]


MINE = (ROWS, NH * DH)


def own_video(scal, vq, vg, ak, av, vstat):
    part = ((2, ROWS, WIDE), BF16)
    scratch = [pltpu.VMEM((3, CH, ROWS), BF16)] * 2 + [pltpu.VMEM((NH, DH, ROWS), F32)]
    scratch += [pltpu.VMEM((2, 2, ROWS, WIDE), BF16)]
    return call(
        own_video_kernel, 5, [part, part, (MINE, F32)], scratch, 28, 20, "own_video",
        scal, vq, vg, ak, av, vstat,
    )


def own_audio(scal, vk, vv, aq, ag, astat):
    part = ((1, ROWS, WIDE), BF16)
    scratch = [pltpu.VMEM((3, ROWS, CH), BF16)] * 2 + [pltpu.VMEM((2, 1, ROWS, WIDE), BF16)]
    return call(
        own_audio_kernel, 5, [part, part, (MINE, F32), (MINE, F32)], scratch, 28, 20, "own_audio",
        scal, vk, vv, aq, ag, astat,
    )


def collect(scal, pieces, audio, which):
    for d in range(4):
        y = lax.rem(scal[S_Y] + 4 - d, 4)
        for swapped in range(2):
            core = scal[S_CORE] if swapped == 0 else 1 - scal[S_CORE]
            row = pl.multiple_of(y * 128 + core * SHARE, SHARE)
            for at, k in enumerate(which):
                audio[at, pl.ds(row, SHARE), :] = pieces[2 * d + swapped][k]


def other_video_kernel(scal, vq, vg, vstat, pvq, *refs):
    pieces, (dvq, audio, prob, dscore, acc) = refs[:8], refs[8:]
    half = 1 - scal[S_AUD]
    collect(scal, pieces, audio, (1, 2))
    acc[...] = jnp.zeros_like(acc)

    def chunk(q, rows):
        def head(h, u):
            hc = head_cols(0, h)
            ak, av = audio[0, rows, hc], audio[1, rows, hc]
            video_queries(scal, half, q, h, ak, av, vq[:, hc], vg[:, hc], vstat, prob.at[u], dscore.at[u])
            acc[h] += dot_nn(ak.T, dscore[u])

        each_head(head, 2)

    each_chunk(scal, half, chunk)

    @pl.loop(0, NH)
    def _(h):
        hc = head_cols(0, h)
        dvq[:, hc] = (pvq[:, hc] + acc[h].T).astype(BF16)


def other_audio_kernel(scal, vk, vv, astat, pvk, pvv, *refs):
    pieces, (dvk, dvv, audio, prob, dscore, acck, accv) = refs[:8], refs[8:]
    half = 1 - scal[S_AUD]
    collect(scal, pieces, audio, (0, 3))
    acck[...] = pvk[...]
    accv[...] = pvv[...]

    def chunk(q, rows):
        def head(h, u):
            hc = head_cols(0, h)
            aq, ag = audio[0, rows, hc], audio[1, rows, hc]
            audio_queries(scal, half, q, h, aq, ag, vk[:, hc], vv[:, hc], astat, prob.at[u], dscore.at[u])
            acck[:, hc] += dot_nn(dscore[u], aq)
            accv[:, hc] += dot_nn(prob[u], ag)

        each_head(head, 2)

    each_chunk(scal, half, chunk)
    dvk[...] = acck[...].astype(BF16)
    dvv[...] = accv[...].astype(BF16)


def other_video(scal, vq, vg, vstat, pvq, pieces):
    scratch = [pltpu.VMEM((2,) + MINE, BF16)] + [pltpu.VMEM((2, CH, ROWS), BF16)] * 2
    scratch += [pltpu.VMEM((NH, DH, ROWS), F32)]
    return call(
        other_video_kernel, 12, [(MINE, BF16)], scratch, 28, 20, "other_video",
        scal, vq, vg, vstat, pvq, *pieces,
    )[0]


def other_audio(scal, vk, vv, astat, pvk, pvv, pieces):
    scratch = [pltpu.VMEM((2,) + MINE, BF16)] + [pltpu.VMEM((2, ROWS, CH), BF16)] * 2
    scratch += [pltpu.VMEM(MINE, F32)] * 2
    return call(
        other_audio_kernel, 13, [(MINE, BF16), (MINE, BF16)], scratch, 28, 20, "other_audio",
        scal, vk, vv, astat, pvk, pvv, *pieces,
    )


def shift(x, axis, d):
    return lax.ppermute(x, axis, [(i, (i + d) % 4) for i in range(4)])


def swap(x, axis):
    return lax.ppermute(x, axis, [(0, 1), (1, 0)])


def along(x, axis, held=None):
    return [x if held is None else after(x, held)] + [shift(x, axis, d) for d in (1, 2, 3)]


def shards(cut, axis):
    return [cut[0]] + [shift(cut[d], axis, d) for d in (1, 2, 3)]


def both_cores(parts):
    return [p for part in parts for p in (part, swap(part, "core"))]


def after(x, *others):
    return lax.optimization_barrier((x, *others))[0]


def add_kernel(groups, axis, size, scal, *refs):
    outs = refs[sum(groups) :]
    at = 0
    first = 0
    for count in groups:
        ins = refs[at : at + count]
        n = ins[0].shape[0]
        for d, out in enumerate(outs):
            if size is None:
                rows = slice(None)
            else:
                rows = pl.ds(pl.multiple_of(lax.rem(scal[axis] + d, 4) * size, size), size)
            total = sum(r[:, rows, :].astype(F32) for r in ins)
            out[first : first + n] = total.astype(BF16)
        at += count
        first += n


def add_and_cut(scal, groups, axis):
    parts = [part for group in groups for part in group]
    n = sum(group[0].shape[0] for group in groups)
    _, rows, width = parts[0].shape
    size = None if axis is None else rows // 4
    outs = 1 if axis is None else 4
    shape = jax.ShapeDtypeStruct((n, rows if axis is None else size, width), BF16)
    return pl.pallas_call(
        functools.partial(add_kernel, [len(group) for group in groups], axis, size),
        in_specs=[pl.BlockSpec(memory_space=pltpu.SMEM)] + [pl.BlockSpec(memory_space=pltpu.VMEM)] * len(parts),
        out_specs=[pl.BlockSpec(memory_space=pltpu.VMEM)] * outs,
        out_shape=[shape] * outs,
        compiler_params=limit(8),
        cost_estimate=cost(1),
        name="add_and_cut",
    )(scal, *parts)


def place_kernel(n, scal, *refs):
    pieces, outs = refs[:8], refs[8:]
    for d in range(4):
        y = lax.rem(scal[S_Y] + 4 - d, 4)
        for swapped in range(2):
            core = scal[S_CORE] if swapped == 0 else 1 - scal[S_CORE]
            cols = pl.ds(pl.multiple_of(core * (HALF * DH), HALF * DH), HALF * DH)
            for e in range(4):
                z = lax.rem(scal[S_Z] + 4 - e, 4)
                row = pl.multiple_of(y * 128 + z * 32, 32)
                for k in range(n):
                    outs[k][pl.ds(row, 32), cols] = pieces[2 * d + swapped][e, k]


def place(scal, pieces):
    n = pieces[0].shape[1]
    shape = jax.ShapeDtypeStruct((ROWS, NH * DH), BF16)
    return pl.pallas_call(
        functools.partial(place_kernel, n),
        in_specs=[pl.BlockSpec(memory_space=pltpu.SMEM)] + [pl.BlockSpec(memory_space=pltpu.VMEM)] * 8,
        out_specs=[pl.BlockSpec(memory_space=pltpu.VMEM)] * n,
        out_shape=[shape] * n,
        compiler_params=limit(8),
        cost_estimate=cost(1),
        name="place",
    )(scal, *pieces)


def per_device(vq, vk, vv, vg, aq, ak, av, ag, alignment):
    y, z, core, aud = (lax.axis_index(name) for name in ("y", "z", "core", "aud"))
    vid = (y * 4 + z) * 2 + core
    mask = lax.dynamic_slice(alignment, (vid * 4, 0), (4, 16)).reshape(64)
    scal = jnp.concatenate([jnp.stack([y, z, core, aud]).astype(jnp.int32), mask])

    apart, share = statistics(audio_stats_kernel, "audio_stats", 2, scal, vk, vv, aq, ag)
    vpart, share = statistics(video_stats_kernel, "video_stats", 4, after(scal, apart), vq, vg, ak, av, share)
    apart = merge(scal, [after(apart, vpart), swap(apart, "core")], False)
    apart = merge(scal, along(apart, "z"), False)
    vstat = merge(scal, [vpart, swap(vpart, "aud")], True)
    keep_v, send_v, dvq = own_video(after(scal, apart), vq, vg, ak, av, vstat)
    astat = merge(scal, along(apart, "y", dvq), True)
    share = swap(after(share, astat), "aud")
    keep_a, send_a, dvk, dvv = own_audio(scal, vk, vv, aq, ag, astat)
    share = after(share, dvk)
    cut = add_and_cut(scal, [[keep_v, swap(send_v, "core")], [keep_a, swap(send_a, "core")]], S_Y)
    astat_other = swap(after(astat, cut[0]), "aud")
    cut = add_and_cut(scal, [shards(cut, "y")], S_Z)
    share = after(share, cut[0])
    own, first, third = share, shift(share, "y", 1), shift(share, "y", 3)
    shards_z = shards(cut, "z")
    piece = add_and_cut(scal, [[after(shards_z[0], astat_other)] + shards_z[1:]], None)[0]
    second = shift(after(share, piece), "y", 2)
    line = jnp.stack(along(after(piece, first, third), "z"))
    pieces = both_cores([own, first, after(second, line), third])
    dvq = other_video(after(scal, line), vq, vg, vstat, dvq, pieces)
    dvk, dvv = other_audio(after(scal, dvq), vk, vv, astat_other, dvk, dvv, pieces)
    gathered = along(line, "y")
    gathered = both_cores(gathered[:1]) + both_cores([after(part, dvk) for part in gathered[1:]])
    dak, dav, daq = place(scal, gathered)
    return dvq, dvk, dvv, daq, dak, dav


def solution(mesh):
    grid = Mesh(mesh.devices.reshape(4, 4, 2, 2, 4), ("y", "z", "core", "aud", "head"))
    video = P(("y", "z", "core"), "head")
    audio = P("aud", "head")
    return jax.shard_map(
        per_device,
        mesh=grid,
        in_specs=(video,) * 4 + (audio,) * 4 + (P(),),
        out_specs=(video,) * 3 + (audio,) * 3,
        check_vma=False,
    )
```

```python
import functools
import math

import jax
import jax.numpy as jnp
from jax import lax
from jax.experimental import pallas as pl
from jax.experimental.pallas import tpu as pltpu
from jax.sharding import Mesh
from jax.sharding import PartitionSpec as P

DH = 128
VBLK = 128
ABLK = 64
NH = 6
HALF = 3
ROWS = 512
CH = 256
SHARE = 64
SCALE = DH ** -0.5
C2 = SCALE * math.log2(math.e)
MASKED = -1e30
FLOOR = -1e29
WIDE = HALF * DH
F32 = jnp.float32
BF16 = jnp.bfloat16
STAT = ((3, 8, ROWS), F32)
BOTH = ((2, 8, ROWS), F32)

S_Y, S_Z, S_CORE, S_AUD, S_MASK = 0, 1, 2, 3, 4

MIB = 1024 * 1024


def cost(us):
    return pl.CostEstimate(flops=us * 1_000_000_000, bytes_accessed=100_000, transcendentals=0)


def limit(mib):
    return pltpu.CompilerParams(vmem_limit_bytes=mib * MIB)


def call(kernel, ins, outs, scratch, mib, us, name, scal, *arrays):
    vmem = pl.BlockSpec(memory_space=pltpu.VMEM)
    return pl.pallas_call(
        kernel,
        in_specs=[pl.BlockSpec(memory_space=pltpu.SMEM)] + [vmem] * ins,
        out_specs=[vmem] * len(outs),
        out_shape=[jax.ShapeDtypeStruct(shape, dtype) for shape, dtype in outs],
        scratch_shapes=scratch,
        compiler_params=limit(mib),
        cost_estimate=cost(us),
        name=name,
    )(scal, *arrays)


def dot_nt(a, b):
    return lax.dot_general(a, b, (((1,), (1,)), ((), ())), preferred_element_type=F32)


def dot_nn(a, b):
    return lax.dot_general(a, b, (((1,), (0,)), ((), ())), preferred_element_type=F32)


def bias_of(scal, half, i, j):
    return jnp.where(scal[S_MASK + i * 16 + half * 8 + j] > 0, 0.0, MASKED)


def chunk_active(scal, half, q):
    c = scal[S_Y] * 4 + scal[S_Z]
    first = half * 8 + q * (CH // ABLK)
    return jnp.logical_and(first <= c + 3, first + CH // ABLK - 1 >= c - 3)


def each_chunk(scal, half, body, idle=None):
    @pl.loop(0, ROWS // CH)
    def _(q):
        rows = pl.ds(pl.multiple_of(q * CH, CH), CH)
        active = chunk_active(scal, half, q)

        @pl.when(active)
        def _():
            body(q, rows)

        if idle is not None:

            @pl.when(jnp.logical_not(active))
            def _():
                idle(rows)


def each_head(body, together):
    @pl.loop(0, NH // together)
    def _(p):
        for u in range(together):
            body(together * p + u, u)


def pair_bias(scal, half, i, j):
    lane = lax.broadcasted_iota(jnp.int32, (1, 128), 1)
    return jnp.where(lane < ABLK, bias_of(scal, half, i, j), bias_of(scal, half, i, j + 1))


def head_cols(g, r):
    return pl.ds(pl.multiple_of(g * WIDE + r * DH, DH), DH)


def first_rows(held):
    for h in range(NH):
        held[h, 0:1, :] = jnp.full((1, ROWS), FLOOR, F32)
        held[h, 1:2, :] = jnp.zeros((1, ROWS), F32)
        held[h, 2:3, :] = jnp.zeros((1, ROWS), F32)


def store_rows(stat, held):
    for k in range(3):
        for h in range(NH):
            stat[k, h : h + 1, :] = held[h, k : k + 1, :]
        stat[k, NH:8, :] = jnp.ones((8 - NH, ROWS), F32)


def shared_rows(scal):
    return pl.ds(pl.multiple_of(scal[S_Y] * 128 + scal[S_CORE] * SHARE, SHARE), SHARE)


def audio_stats_kernel(scal, vk, vv, aq, ag, stat, share, held):
    half = scal[S_AUD]
    first_rows(held)

    def chunk(q, rows):
        bias = [[pair_bias(scal, half, i, q * 4 + jj * 2) for i in range(4)] for jj in range(2)]

        def head(h, u):
            hc = head_cols(0, h)
            s = dot_nt(vk[:, hc], aq[rows, hc])
            t = dot_nt(vv[:, hc], ag[rows, hc])
            for jj in range(CH // 128):
                cols = slice(jj * 128, (jj + 1) * 128)
                out = pl.ds(pl.multiple_of(q * CH + jj * 128, 128), 128)
                top = jnp.full((1, 128), FLOOR, F32)
                for i in range(4):
                    best = jnp.max(s[i * 128 : (i + 1) * 128, cols], axis=0, keepdims=True)
                    top = jnp.maximum(top, best * C2 + bias[jj][i])
                total = jnp.zeros((1, 128), F32)
                part = jnp.zeros((1, 128), F32)
                for i in range(4):
                    e = jnp.exp2(s[i * 128 : (i + 1) * 128, cols] * C2 - (top - bias[jj][i]))
                    total += jnp.sum(e, axis=0, keepdims=True)
                    part += jnp.sum(e * t[i * 128 : (i + 1) * 128, cols], axis=0, keepdims=True)
                held[h, 0:1, out] = top
                held[h, 1:2, out] = total
                held[h, 2:3, out] = part

        each_head(head, 3)

    each_chunk(scal, half, chunk)
    store_rows(stat, held)
    rows = shared_rows(scal)
    share[0] = aq[rows, :]
    share[1] = ag[rows, :]


def video_stats_kernel(scal, vq, vg, ak, av, audio_share, stat, share, held):
    half = scal[S_AUD]
    first_rows(held)

    def chunk(q, rows):
        bias = [[bias_of(scal, half, i, q * 4 + j) for j in range(4)] for i in range(4)]

        def head(h, u):
            hc = head_cols(0, h)
            s = dot_nt(ak[rows, hc], vq[:, hc])
            t = dot_nt(av[rows, hc], vg[:, hc])
            for i in range(4):
                cols = slice(i * 128, (i + 1) * 128)
                old = held[h, 0:1, cols]
                top = old
                for j in range(4):
                    best = jnp.max(s[j * 64 : (j + 1) * 64, cols], axis=0, keepdims=True)
                    top = jnp.maximum(top, best * C2 + bias[i][j])
                shrink = jnp.exp2(old - top)
                total = held[h, 1:2, cols] * shrink
                part = held[h, 2:3, cols] * shrink
                for j in range(4):
                    e = jnp.exp2(s[j * 64 : (j + 1) * 64, cols] * C2 - (top - bias[i][j]))
                    total += jnp.sum(e, axis=0, keepdims=True)
                    part += jnp.sum(e * t[j * 64 : (j + 1) * 64, cols], axis=0, keepdims=True)
                held[h, 0:1, cols] = top
                held[h, 1:2, cols] = total
                held[h, 2:3, cols] = part

        each_head(head, 3)

    each_chunk(scal, half, chunk)
    store_rows(stat, held)
    rows = shared_rows(scal)
    share[0] = audio_share[0]
    share[1] = ak[rows, :]
    share[2] = av[rows, :]
    share[3] = audio_share[1]


def statistics(kernel, name, shared, scal, *arrays):
    scratch = [pltpu.VMEM((NH, 8, ROWS), F32)]
    share = ((shared, SHARE, NH * DH), BF16)
    return call(kernel, len(arrays), [STAT, share], scratch, 24, 20, name, scal, *arrays)


def merge_kernel(final, scal, *refs):
    *ins, out = refs
    tops = [r[0] for r in ins]
    top = functools.reduce(jnp.maximum, tops)
    weights = [jnp.exp2(t - top) for t in tops]
    total = sum(r[1] * w for r, w in zip(ins, weights))
    part = sum(r[2] * w for r, w in zip(ins, weights))
    if final:
        out[0] = top + jnp.log(total) * math.log2(math.e)
        out[1] = part / total
    else:
        out[0] = top
        out[1] = total
        out[2] = part


def merge(scal, stats, final):
    kernel = functools.partial(merge_kernel, final)
    return call(kernel, len(stats), [BOTH if final else STAT], [], 4, 1, "merge", scal, *stats)[0]


def video_queries(scal, half, q, h, ak, av, vq, vg, vstat, prob, dscore):
    s = dot_nt(ak, vq)
    t = dot_nt(av, vg)
    lses = vstat[0, pl.ds(h, 1), :]
    deltas = vstat[1, pl.ds(h, 1), :]
    for i in range(4):
        cols = slice(i * 128, (i + 1) * 128)
        lse, delta = lses[:, cols], deltas[:, cols]
        for j in range(4):
            rows = slice(j * 64, (j + 1) * 64)
            p = jnp.exp2(s[rows, cols] * C2 - (lse - bias_of(scal, half, i, q * 4 + j)))
            prob[rows, cols] = p.astype(BF16)
            dscore[rows, cols] = (p * (t[rows, cols] - delta) * SCALE).astype(BF16)


def audio_queries(scal, half, q, h, aq, ag, vk, vv, astat, prob, dscore):
    s = dot_nt(vk, aq)
    t = dot_nt(vv, ag)
    lses = astat[0, pl.ds(h, 1), :]
    deltas = astat[1, pl.ds(h, 1), :]
    for jj in range(CH // 128):
        cols = slice(jj * 128, (jj + 1) * 128)
        first, second = slice(jj * 128, jj * 128 + 128), slice(CH + jj * 128, CH + jj * 128 + 128)
        lse = jnp.where(q == 0, lses[:, first], lses[:, second])
        delta = jnp.where(q == 0, deltas[:, first], deltas[:, second])
        for i in range(4):
            rows = slice(i * 128, (i + 1) * 128)
            p = jnp.exp2(s[rows, cols] * C2 - (lse - pair_bias(scal, half, i, q * 4 + jj * 2)))
            prob[rows, cols] = p.astype(BF16)
            dscore[rows, cols] = (p * (t[rows, cols] - delta) * SCALE).astype(BF16)


def own_head(scal, at):
    h = lax.rem(scal[S_CORE] * HALF + at, NH)
    return h, head_cols(0, h), at // HALF, head_cols(0, lax.rem(at, HALF))


def own_video_kernel(scal, vq, vg, ak, av, vstat, keep, send, dvq, prob, dscore, acc, sums):
    half = scal[S_AUD]
    acc[...] = jnp.zeros_like(acc)

    def chunk(q, rows):
        def head(at, u):
            h, hc, step, sc = own_head(scal, at)
            video_queries(
                scal, half, q, h, ak[rows, hc], av[rows, hc], vq[:, hc], vg[:, hc], vstat, prob.at[u], dscore.at[u]
            )
            ds = dscore[u]
            sums[step, 0, rows, sc] = dot_nn(ds, vq[:, hc]).astype(BF16)
            sums[step, 1, rows, sc] = dot_nn(prob[u], vg[:, hc]).astype(BF16)
            acc[at] += dot_nn(ak[rows, hc].T, ds)

        each_head(head, 3)

    def idle(rows):
        for step in range(2):
            for k in range(2):
                sums[step, k, rows, :] = jnp.zeros((CH, WIDE), BF16)

    each_chunk(scal, half, chunk, idle)
    keep[...] = sums[0]
    send[...] = sums[1]

    @pl.loop(0, NH)
    def _(at):
        dvq[:, own_head(scal, at)[1]] = acc[at].T


def own_audio_kernel(scal, vk, vv, aq, ag, astat, keep, send, dvk, dvv, prob, dscore, sums):
    half = scal[S_AUD]
    dvk[...] = jnp.zeros_like(dvk)
    dvv[...] = jnp.zeros_like(dvv)

    def chunk(q, rows):
        def head(at, u):
            h, hc, step, sc = own_head(scal, at)
            audio_queries(
                scal, half, q, h, aq[rows, hc], ag[rows, hc], vk[:, hc], vv[:, hc], astat, prob.at[u], dscore.at[u]
            )
            ds = dscore[u]
            sums[step, 0, rows, sc] = dot_nn(vk[:, hc].T, ds).T.astype(BF16)
            dvk[:, hc] += dot_nn(ds, aq[rows, hc])
            dvv[:, hc] += dot_nn(prob[u], ag[rows, hc])

        each_head(head, 3)

    def idle(rows):
        for step in range(2):
            sums[step, 0, rows, :] = jnp.zeros((CH, WIDE), BF16)

    each_chunk(scal, half, chunk, idle)
    keep[...] = sums[0]
    send[...] = sums[1]


MINE = (ROWS, NH * DH)


def own_video(scal, vq, vg, ak, av, vstat):
    part = ((2, ROWS, WIDE), BF16)
    scratch = [pltpu.VMEM((3, CH, ROWS), BF16)] * 2 + [pltpu.VMEM((NH, DH, ROWS), F32)]
    scratch += [pltpu.VMEM((2, 2, ROWS, WIDE), BF16)]
    return call(
        own_video_kernel, 5, [part, part, (MINE, F32)], scratch, 28, 20, "own_video",
        scal, vq, vg, ak, av, vstat,
    )


def own_audio(scal, vk, vv, aq, ag, astat):
    part = ((1, ROWS, WIDE), BF16)
    scratch = [pltpu.VMEM((3, ROWS, CH), BF16)] * 2 + [pltpu.VMEM((2, 1, ROWS, WIDE), BF16)]
    return call(
        own_audio_kernel, 5, [part, part, (MINE, F32), (MINE, F32)], scratch, 28, 20, "own_audio",
        scal, vk, vv, aq, ag, astat,
    )


def collect(scal, pieces, audio, which):
    for d in range(4):
        y = lax.rem(scal[S_Y] + 4 - d, 4)
        for swapped in range(2):
            core = scal[S_CORE] if swapped == 0 else 1 - scal[S_CORE]
            row = pl.multiple_of(y * 128 + core * SHARE, SHARE)
            for at, k in enumerate(which):
                audio[at, pl.ds(row, SHARE), :] = pieces[2 * d + swapped][k]


def other_video_kernel(scal, vq, vg, vstat, pvq, *refs):
    pieces, (dvq, audio, prob, dscore, acc) = refs[:8], refs[8:]
    half = 1 - scal[S_AUD]
    collect(scal, pieces, audio, (1, 2))
    acc[...] = jnp.zeros_like(acc)

    def chunk(q, rows):
        def head(h, u):
            hc = head_cols(0, h)
            ak, av = audio[0, rows, hc], audio[1, rows, hc]
            video_queries(scal, half, q, h, ak, av, vq[:, hc], vg[:, hc], vstat, prob.at[u], dscore.at[u])
            acc[h] += dot_nn(ak.T, dscore[u])

        each_head(head, 2)

    each_chunk(scal, half, chunk)

    @pl.loop(0, NH)
    def _(h):
        hc = head_cols(0, h)
        dvq[:, hc] = (pvq[:, hc] + acc[h].T).astype(BF16)


def other_audio_kernel(scal, vk, vv, astat, pvk, pvv, *refs):
    pieces, (dvk, dvv, audio, prob, dscore, acck, accv) = refs[:8], refs[8:]
    half = 1 - scal[S_AUD]
    collect(scal, pieces, audio, (0, 3))
    acck[...] = pvk[...]
    accv[...] = pvv[...]

    def chunk(q, rows):
        def head(h, u):
            hc = head_cols(0, h)
            aq, ag = audio[0, rows, hc], audio[1, rows, hc]
            audio_queries(scal, half, q, h, aq, ag, vk[:, hc], vv[:, hc], astat, prob.at[u], dscore.at[u])
            acck[:, hc] += dot_nn(dscore[u], aq)
            accv[:, hc] += dot_nn(prob[u], ag)

        each_head(head, 2)

    each_chunk(scal, half, chunk)
    dvk[...] = acck[...].astype(BF16)
    dvv[...] = accv[...].astype(BF16)


def other_video(scal, vq, vg, vstat, pvq, pieces):
    scratch = [pltpu.VMEM((2,) + MINE, BF16)] + [pltpu.VMEM((2, CH, ROWS), BF16)] * 2
    scratch += [pltpu.VMEM((NH, DH, ROWS), F32)]
    return call(
        other_video_kernel, 12, [(MINE, BF16)], scratch, 28, 20, "other_video",
        scal, vq, vg, vstat, pvq, *pieces,
    )[0]


def other_audio(scal, vk, vv, astat, pvk, pvv, pieces):
    scratch = [pltpu.VMEM((2,) + MINE, BF16)] + [pltpu.VMEM((2, ROWS, CH), BF16)] * 2
    scratch += [pltpu.VMEM(MINE, F32)] * 2
    return call(
        other_audio_kernel, 13, [(MINE, BF16), (MINE, BF16)], scratch, 28, 20, "other_audio",
        scal, vk, vv, astat, pvk, pvv, *pieces,
    )


def shift(x, axis, d):
    return lax.ppermute(x, axis, [(i, (i + d) % 4) for i in range(4)])


def swap(x, axis):
    return lax.ppermute(x, axis, [(0, 1), (1, 0)])


def along(x, axis, held=None):
    return [x if held is None else after(x, held)] + [shift(x, axis, d) for d in (1, 2, 3)]


def shards(cut, axis):
    return [cut[0]] + [shift(cut[d], axis, d) for d in (1, 2, 3)]


def both_cores(parts):
    return [p for part in parts for p in (part, swap(part, "core"))]


def after(x, *others):
    return lax.optimization_barrier((x, *others))[0]


def add_kernel(groups, axis, size, scal, *refs):
    outs = refs[sum(groups) :]
    at = 0
    first = 0
    for count in groups:
        ins = refs[at : at + count]
        n = ins[0].shape[0]
        for d, out in enumerate(outs):
            if size is None:
                rows = slice(None)
            else:
                rows = pl.ds(pl.multiple_of(lax.rem(scal[axis] + d, 4) * size, size), size)
            total = sum(r[:, rows, :].astype(F32) for r in ins)
            out[first : first + n] = total.astype(BF16)
        at += count
        first += n


def add_and_cut(scal, groups, axis):
    parts = [part for group in groups for part in group]
    n = sum(group[0].shape[0] for group in groups)
    _, rows, width = parts[0].shape
    size = None if axis is None else rows // 4
    outs = 1 if axis is None else 4
    shape = jax.ShapeDtypeStruct((n, rows if axis is None else size, width), BF16)
    return pl.pallas_call(
        functools.partial(add_kernel, [len(group) for group in groups], axis, size),
        in_specs=[pl.BlockSpec(memory_space=pltpu.SMEM)] + [pl.BlockSpec(memory_space=pltpu.VMEM)] * len(parts),
        out_specs=[pl.BlockSpec(memory_space=pltpu.VMEM)] * outs,
        out_shape=[shape] * outs,
        compiler_params=limit(8),
        cost_estimate=cost(1),
        name="add_and_cut",
    )(scal, *parts)


def place_kernel(n, scal, *refs):
    pieces, outs = refs[:8], refs[8:]
    for d in range(4):
        y = lax.rem(scal[S_Y] + 4 - d, 4)
        for swapped in range(2):
            core = scal[S_CORE] if swapped == 0 else 1 - scal[S_CORE]
            cols = pl.ds(pl.multiple_of(core * (HALF * DH), HALF * DH), HALF * DH)
            for e in range(4):
                z = lax.rem(scal[S_Z] + 4 - e, 4)
                row = pl.multiple_of(y * 128 + z * 32, 32)
                for k in range(n):
                    outs[k][pl.ds(row, 32), cols] = pieces[2 * d + swapped][e, k]


def place(scal, pieces):
    n = pieces[0].shape[1]
    shape = jax.ShapeDtypeStruct((ROWS, NH * DH), BF16)
    return pl.pallas_call(
        functools.partial(place_kernel, n),
        in_specs=[pl.BlockSpec(memory_space=pltpu.SMEM)] + [pl.BlockSpec(memory_space=pltpu.VMEM)] * 8,
        out_specs=[pl.BlockSpec(memory_space=pltpu.VMEM)] * n,
        out_shape=[shape] * n,
        compiler_params=limit(8),
        cost_estimate=cost(1),
        name="place",
    )(scal, *pieces)


def per_device(vq, vk, vv, vg, aq, ak, av, ag, alignment):
    y, z, core, aud = (lax.axis_index(name) for name in ("y", "z", "core", "aud"))
    vid = (y * 4 + z) * 2 + core
    mask = lax.dynamic_slice(alignment, (vid * 4, 0), (4, 16)).reshape(64)
    scal = jnp.concatenate([jnp.stack([y, z, core, aud]).astype(jnp.int32), mask])

    apart, share = statistics(audio_stats_kernel, "audio_stats", 2, scal, vk, vv, aq, ag)
    vpart, share = statistics(video_stats_kernel, "video_stats", 4, after(scal, apart), vq, vg, ak, av, share)
    apart = merge(scal, [after(apart, vpart), swap(apart, "core")], False)
    apart = merge(scal, along(apart, "z"), False)
    vstat = merge(scal, [vpart, swap(vpart, "aud")], True)
    keep_v, send_v, dvq = own_video(after(scal, apart), vq, vg, ak, av, vstat)
    astat = merge(scal, along(apart, "y", dvq), True)
    share = swap(after(share, astat), "aud")
    astat_other = swap(astat, "aud")
    keep_a, send_a, dvk, dvv = own_audio(scal, vk, vv, aq, ag, astat)
    share = after(share, dvk)
    send_a = after(send_a, astat_other)
    cut = add_and_cut(scal, [[keep_v, swap(send_v, "core")], [keep_a, swap(send_a, "core")]], S_Y)
    shards_y = shards(cut, "y")
    cut = add_and_cut(scal, [shards_y], S_Z)
    share = after(share, shards_y[1])
    own, first, third = share, shift(share, "y", 1), shift(share, "y", 3)
    shards_z = shards(cut, "z")
    piece = add_and_cut(scal, [shards_z], None)[0]
    second = shift(after(share, piece), "y", 2)
    line = jnp.stack(along(after(piece, first, third), "z"))
    pieces = both_cores([own, first, after(second, line), third])
    dvq = other_video(after(scal, line), vq, vg, vstat, dvq, pieces)
    dvk, dvv = other_audio(after(scal, dvq), vk, vv, astat_other, dvk, dvv, pieces)
    gathered = along(line, "y")
    gathered = both_cores(gathered[:1]) + both_cores([after(part, dvk) for part in gathered[1:]])
    dak, dav, daq = place(scal, gathered)
    return dvq, dvk, dvv, daq, dak, dav


def solution(mesh):
    grid = Mesh(mesh.devices.reshape(4, 4, 2, 2, 4), ("y", "z", "core", "aud", "head"))
    video = P(("y", "z", "core"), "head")
    audio = P("aud", "head")
    return jax.shard_map(
        per_device,
        mesh=grid,
        in_specs=(video,) * 4 + (audio,) * 4 + (P(),),
        out_specs=(video,) * 3 + (audio,) * 3,
        check_vma=False,
    )
```

```python
import functools
import math

import jax
import jax.numpy as jnp
from jax import lax
from jax.experimental import pallas as pl
from jax.experimental.pallas import tpu as pltpu
from jax.sharding import Mesh
from jax.sharding import PartitionSpec as P

DH = 128
VBLK = 128
ABLK = 64
NH = 6
HALF = 3
ROWS = 512
CH = 256
SHARE = 64
SCALE = DH ** -0.5
C2 = SCALE * math.log2(math.e)
MASKED = -1e30
FLOOR = -1e29
WIDE = HALF * DH
F32 = jnp.float32
BF16 = jnp.bfloat16
STAT = ((3, 8, ROWS), F32)
BOTH = ((2, 8, ROWS), F32)

S_Y, S_Z, S_CORE, S_AUD, S_MASK = 0, 1, 2, 3, 4

MIB = 1024 * 1024


def cost(us):
    return pl.CostEstimate(flops=us * 1_000_000_000, bytes_accessed=100_000, transcendentals=0)


def limit(mib):
    return pltpu.CompilerParams(vmem_limit_bytes=mib * MIB)


def call(kernel, ins, outs, scratch, mib, us, name, scal, *arrays):
    vmem = pl.BlockSpec(memory_space=pltpu.VMEM)
    return pl.pallas_call(
        kernel,
        in_specs=[pl.BlockSpec(memory_space=pltpu.SMEM)] + [vmem] * ins,
        out_specs=[vmem] * len(outs),
        out_shape=[jax.ShapeDtypeStruct(shape, dtype) for shape, dtype in outs],
        scratch_shapes=scratch,
        compiler_params=limit(mib),
        cost_estimate=cost(us),
        name=name,
    )(scal, *arrays)


def dot_nt(a, b):
    return lax.dot_general(a, b, (((1,), (1,)), ((), ())), preferred_element_type=F32)


def dot_nn(a, b):
    return lax.dot_general(a, b, (((1,), (0,)), ((), ())), preferred_element_type=F32)


def bias_of(scal, half, i, j):
    return jnp.where(scal[S_MASK + i * 16 + half * 8 + j] > 0, 0.0, MASKED)


def chunk_active(scal, half, q):
    c = scal[S_Y] * 4 + scal[S_Z]
    first = half * 8 + q * (CH // ABLK)
    return jnp.logical_and(first <= c + 3, first + CH // ABLK - 1 >= c - 3)


def each_chunk(scal, half, body, idle=None):
    @pl.loop(0, ROWS // CH)
    def _(q):
        rows = pl.ds(pl.multiple_of(q * CH, CH), CH)
        active = chunk_active(scal, half, q)

        @pl.when(active)
        def _():
            body(q, rows)

        if idle is not None:

            @pl.when(jnp.logical_not(active))
            def _():
                idle(rows)


def each_head(body, together):
    @pl.loop(0, NH // together)
    def _(p):
        for u in range(together):
            body(together * p + u, u)


def pair_bias(scal, half, i, j):
    lane = lax.broadcasted_iota(jnp.int32, (1, 128), 1)
    return jnp.where(lane < ABLK, bias_of(scal, half, i, j), bias_of(scal, half, i, j + 1))


def head_cols(g, r):
    return pl.ds(pl.multiple_of(g * WIDE + r * DH, DH), DH)


def first_rows(held):
    for h in range(NH):
        held[h, 0:1, :] = jnp.full((1, ROWS), FLOOR, F32)
        held[h, 1:2, :] = jnp.zeros((1, ROWS), F32)
        held[h, 2:3, :] = jnp.zeros((1, ROWS), F32)


def store_rows(stat, held):
    for k in range(3):
        for h in range(NH):
            stat[k, h : h + 1, :] = held[h, k : k + 1, :]
        stat[k, NH:8, :] = jnp.ones((8 - NH, ROWS), F32)


def shared_rows(scal):
    return pl.ds(pl.multiple_of(scal[S_Y] * 128 + scal[S_CORE] * SHARE, SHARE), SHARE)


def audio_stats_kernel(scal, vk, vv, aq, ag, stat, share, held):
    half = scal[S_AUD]
    first_rows(held)

    def chunk(q, rows):
        bias = [[pair_bias(scal, half, i, q * 4 + jj * 2) for i in range(4)] for jj in range(2)]

        def head(h, u):
            hc = head_cols(0, h)
            s = dot_nt(vk[:, hc], aq[rows, hc])
            t = dot_nt(vv[:, hc], ag[rows, hc])
            for jj in range(CH // 128):
                cols = slice(jj * 128, (jj + 1) * 128)
                out = pl.ds(pl.multiple_of(q * CH + jj * 128, 128), 128)
                top = jnp.full((1, 128), FLOOR, F32)
                for i in range(4):
                    best = jnp.max(s[i * 128 : (i + 1) * 128, cols], axis=0, keepdims=True)
                    top = jnp.maximum(top, best * C2 + bias[jj][i])
                total = jnp.zeros((1, 128), F32)
                part = jnp.zeros((1, 128), F32)
                for i in range(4):
                    e = jnp.exp2(s[i * 128 : (i + 1) * 128, cols] * C2 - (top - bias[jj][i]))
                    total += jnp.sum(e, axis=0, keepdims=True)
                    part += jnp.sum(e * t[i * 128 : (i + 1) * 128, cols], axis=0, keepdims=True)
                held[h, 0:1, out] = top
                held[h, 1:2, out] = total
                held[h, 2:3, out] = part

        each_head(head, 3)

    each_chunk(scal, half, chunk)
    store_rows(stat, held)
    rows = shared_rows(scal)
    share[0] = aq[rows, :]
    share[1] = ag[rows, :]


def video_stats_kernel(scal, vq, vg, ak, av, stat, share, held):
    half = scal[S_AUD]
    first_rows(held)

    def chunk(q, rows):
        bias = [[bias_of(scal, half, i, q * 4 + j) for j in range(4)] for i in range(4)]

        def head(h, u):
            hc = head_cols(0, h)
            s = dot_nt(ak[rows, hc], vq[:, hc])
            t = dot_nt(av[rows, hc], vg[:, hc])
            for i in range(4):
                cols = slice(i * 128, (i + 1) * 128)
                old = held[h, 0:1, cols]
                top = old
                for j in range(4):
                    best = jnp.max(s[j * 64 : (j + 1) * 64, cols], axis=0, keepdims=True)
                    top = jnp.maximum(top, best * C2 + bias[i][j])
                shrink = jnp.exp2(old - top)
                total = held[h, 1:2, cols] * shrink
                part = held[h, 2:3, cols] * shrink
                for j in range(4):
                    e = jnp.exp2(s[j * 64 : (j + 1) * 64, cols] * C2 - (top - bias[i][j]))
                    total += jnp.sum(e, axis=0, keepdims=True)
                    part += jnp.sum(e * t[j * 64 : (j + 1) * 64, cols], axis=0, keepdims=True)
                held[h, 0:1, cols] = top
                held[h, 1:2, cols] = total
                held[h, 2:3, cols] = part

        each_head(head, 3)

    each_chunk(scal, half, chunk)
    store_rows(stat, held)
    rows = shared_rows(scal)
    share[0] = ak[rows, :]
    share[1] = av[rows, :]


def statistics(kernel, name, scal, *arrays):
    scratch = [pltpu.VMEM((NH, 8, ROWS), F32)]
    share = ((2, SHARE, NH * DH), BF16)
    return call(kernel, len(arrays), [STAT, share], scratch, 24, 20, name, scal, *arrays)


def merge_kernel(final, scal, *refs):
    *ins, out = refs
    tops = [r[0] for r in ins]
    top = functools.reduce(jnp.maximum, tops)
    weights = [jnp.exp2(t - top) for t in tops]
    total = sum(r[1] * w for r, w in zip(ins, weights))
    part = sum(r[2] * w for r, w in zip(ins, weights))
    if final:
        out[0] = top + jnp.log(total) * math.log2(math.e)
        out[1] = part / total
    else:
        out[0] = top
        out[1] = total
        out[2] = part


def merge(scal, stats, final):
    kernel = functools.partial(merge_kernel, final)
    return call(kernel, len(stats), [BOTH if final else STAT], [], 4, 1, "merge", scal, *stats)[0]


def video_queries(scal, half, q, h, ak, av, vq, vg, vstat, prob, dscore):
    s = dot_nt(ak, vq)
    t = dot_nt(av, vg)
    lses = vstat[0, pl.ds(h, 1), :]
    deltas = vstat[1, pl.ds(h, 1), :]
    for i in range(4):
        cols = slice(i * 128, (i + 1) * 128)
        lse, delta = lses[:, cols], deltas[:, cols]
        for j in range(4):
            rows = slice(j * 64, (j + 1) * 64)
            p = jnp.exp2(s[rows, cols] * C2 - (lse - bias_of(scal, half, i, q * 4 + j)))
            prob[rows, cols] = p.astype(BF16)
            dscore[rows, cols] = (p * (t[rows, cols] - delta) * SCALE).astype(BF16)


def audio_queries(scal, half, q, h, aq, ag, vk, vv, astat, prob, dscore):
    s = dot_nt(vk, aq)
    t = dot_nt(vv, ag)
    lses = astat[0, pl.ds(h, 1), :]
    deltas = astat[1, pl.ds(h, 1), :]
    for jj in range(CH // 128):
        cols = slice(jj * 128, (jj + 1) * 128)
        first, second = slice(jj * 128, jj * 128 + 128), slice(CH + jj * 128, CH + jj * 128 + 128)
        lse = jnp.where(q == 0, lses[:, first], lses[:, second])
        delta = jnp.where(q == 0, deltas[:, first], deltas[:, second])
        for i in range(4):
            rows = slice(i * 128, (i + 1) * 128)
            p = jnp.exp2(s[rows, cols] * C2 - (lse - pair_bias(scal, half, i, q * 4 + jj * 2)))
            prob[rows, cols] = p.astype(BF16)
            dscore[rows, cols] = (p * (t[rows, cols] - delta) * SCALE).astype(BF16)


def own_head(scal, at):
    h = lax.rem(scal[S_CORE] * HALF + at, NH)
    return h, head_cols(0, h), at // HALF, head_cols(0, lax.rem(at, HALF))


def own_video_kernel(scal, vq, vg, ak, av, vstat, keep, send, dvq, prob, dscore, acc, sums):
    half = scal[S_AUD]
    acc[...] = jnp.zeros_like(acc)

    def chunk(q, rows):
        def head(at, u):
            h, hc, step, sc = own_head(scal, at)
            video_queries(
                scal, half, q, h, ak[rows, hc], av[rows, hc], vq[:, hc], vg[:, hc], vstat, prob.at[u], dscore.at[u]
            )
            ds = dscore[u]
            sums[step, 0, rows, sc] = dot_nn(ds, vq[:, hc]).astype(BF16)
            sums[step, 1, rows, sc] = dot_nn(prob[u], vg[:, hc]).astype(BF16)
            acc[at] += dot_nn(ak[rows, hc].T, ds)

        each_head(head, 3)

    def idle(rows):
        for step in range(2):
            for k in range(2):
                sums[step, k, rows, :] = jnp.zeros((CH, WIDE), BF16)

    each_chunk(scal, half, chunk, idle)
    keep[...] = sums[0]
    send[...] = sums[1]

    @pl.loop(0, NH)
    def _(at):
        dvq[:, own_head(scal, at)[1]] = acc[at].T


def own_audio_kernel(scal, vk, vv, aq, ag, astat, keep, send, dvk, dvv, prob, dscore, sums):
    half = scal[S_AUD]
    dvk[...] = jnp.zeros_like(dvk)
    dvv[...] = jnp.zeros_like(dvv)

    def chunk(q, rows):
        def head(at, u):
            h, hc, step, sc = own_head(scal, at)
            audio_queries(
                scal, half, q, h, aq[rows, hc], ag[rows, hc], vk[:, hc], vv[:, hc], astat, prob.at[u], dscore.at[u]
            )
            ds = dscore[u]
            sums[step, 0, rows, sc] = dot_nn(vk[:, hc].T, ds).T.astype(BF16)
            dvk[:, hc] += dot_nn(ds, aq[rows, hc])
            dvv[:, hc] += dot_nn(prob[u], ag[rows, hc])

        each_head(head, 3)

    def idle(rows):
        for step in range(2):
            sums[step, 0, rows, :] = jnp.zeros((CH, WIDE), BF16)

    each_chunk(scal, half, chunk, idle)
    keep[...] = sums[0]
    send[...] = sums[1]


MINE = (ROWS, NH * DH)


def own_video(scal, vq, vg, ak, av, vstat):
    part = ((2, ROWS, WIDE), BF16)
    scratch = [pltpu.VMEM((3, CH, ROWS), BF16)] * 2 + [pltpu.VMEM((NH, DH, ROWS), F32)]
    scratch += [pltpu.VMEM((2, 2, ROWS, WIDE), BF16)]
    return call(
        own_video_kernel, 5, [part, part, (MINE, F32)], scratch, 28, 20, "own_video",
        scal, vq, vg, ak, av, vstat,
    )


def own_audio(scal, vk, vv, aq, ag, astat):
    part = ((1, ROWS, WIDE), BF16)
    scratch = [pltpu.VMEM((3, ROWS, CH), BF16)] * 2 + [pltpu.VMEM((2, 1, ROWS, WIDE), BF16)]
    return call(
        own_audio_kernel, 5, [part, part, (MINE, F32), (MINE, F32)], scratch, 28, 20, "own_audio",
        scal, vk, vv, aq, ag, astat,
    )


def collect(scal, pieces, audio, which):
    for d in range(4):
        y = lax.rem(scal[S_Y] + 4 - d, 4)
        for swapped in range(2):
            core = scal[S_CORE] if swapped == 0 else 1 - scal[S_CORE]
            row = pl.multiple_of(y * 128 + core * SHARE, SHARE)
            for at, k in enumerate(which):
                audio[at, pl.ds(row, SHARE), :] = pieces[2 * d + swapped][k]


def other_video_kernel(scal, vq, vg, vstat, pvq, *refs):
    pieces, (dvq, audio, prob, dscore, acc) = refs[:8], refs[8:]
    half = 1 - scal[S_AUD]
    collect(scal, pieces, audio, (2, 3))
    acc[...] = jnp.zeros_like(acc)

    def chunk(q, rows):
        def head(h, u):
            hc = head_cols(0, h)
            ak, av = audio[0, rows, hc], audio[1, rows, hc]
            video_queries(scal, half, q, h, ak, av, vq[:, hc], vg[:, hc], vstat, prob.at[u], dscore.at[u])
            acc[h] += dot_nn(ak.T, dscore[u])

        each_head(head, 2)

    each_chunk(scal, half, chunk)

    @pl.loop(0, NH)
    def _(h):
        hc = head_cols(0, h)
        dvq[:, hc] = (pvq[:, hc] + acc[h].T).astype(BF16)


def other_audio_kernel(scal, vk, vv, astat, pvk, pvv, *refs):
    pieces, (dvk, dvv, audio, prob, dscore, acck, accv) = refs[:8], refs[8:]
    half = 1 - scal[S_AUD]
    collect(scal, pieces, audio, (0, 1))
    acck[...] = pvk[...]
    accv[...] = pvv[...]

    def chunk(q, rows):
        def head(h, u):
            hc = head_cols(0, h)
            aq, ag = audio[0, rows, hc], audio[1, rows, hc]
            audio_queries(scal, half, q, h, aq, ag, vk[:, hc], vv[:, hc], astat, prob.at[u], dscore.at[u])
            acck[:, hc] += dot_nn(dscore[u], aq)
            accv[:, hc] += dot_nn(prob[u], ag)

        each_head(head, 2)

    each_chunk(scal, half, chunk)
    dvk[...] = acck[...].astype(BF16)
    dvv[...] = accv[...].astype(BF16)


def other_video(scal, vq, vg, vstat, pvq, pieces):
    scratch = [pltpu.VMEM((2,) + MINE, BF16)] + [pltpu.VMEM((2, CH, ROWS), BF16)] * 2
    scratch += [pltpu.VMEM((NH, DH, ROWS), F32)]
    return call(
        other_video_kernel, 12, [(MINE, BF16)], scratch, 28, 20, "other_video",
        scal, vq, vg, vstat, pvq, *pieces,
    )[0]


def other_audio(scal, vk, vv, astat, pvk, pvv, pieces):
    scratch = [pltpu.VMEM((2,) + MINE, BF16)] + [pltpu.VMEM((2, ROWS, CH), BF16)] * 2
    scratch += [pltpu.VMEM(MINE, F32)] * 2
    return call(
        other_audio_kernel, 13, [(MINE, BF16), (MINE, BF16)], scratch, 28, 20, "other_audio",
        scal, vk, vv, astat, pvk, pvv, *pieces,
    )


def shift(x, axis, d):
    return lax.ppermute(x, axis, [(i, (i + d) % 4) for i in range(4)])


def swap(x, axis):
    return lax.ppermute(x, axis, [(0, 1), (1, 0)])


def along(x, axis, held=None):
    return [x if held is None else after(x, held)] + [shift(x, axis, d) for d in (1, 2, 3)]


def shards(cut, axis):
    return [cut[0]] + [shift(cut[d], axis, d) for d in (1, 2, 3)]


def both_cores(parts):
    return [p for part in parts for p in (part, swap(part, "core"))]


def after(x, *others):
    return lax.optimization_barrier((x, *others))[0]


def add_kernel(groups, axis, size, scal, *refs):
    outs = refs[sum(groups) :]
    at = 0
    first = 0
    for count in groups:
        ins = refs[at : at + count]
        n = ins[0].shape[0]
        for d, out in enumerate(outs):
            if size is None:
                rows = slice(None)
            else:
                rows = pl.ds(pl.multiple_of(lax.rem(scal[axis] + d, 4) * size, size), size)
            total = sum(r[:, rows, :].astype(F32) for r in ins)
            out[first : first + n] = total.astype(BF16)
        at += count
        first += n


def add_and_cut(scal, groups, axis):
    parts = [part for group in groups for part in group]
    n = sum(group[0].shape[0] for group in groups)
    _, rows, width = parts[0].shape
    size = None if axis is None else rows // 4
    outs = 1 if axis is None else 4
    shape = jax.ShapeDtypeStruct((n, rows if axis is None else size, width), BF16)
    return pl.pallas_call(
        functools.partial(add_kernel, [len(group) for group in groups], axis, size),
        in_specs=[pl.BlockSpec(memory_space=pltpu.SMEM)] + [pl.BlockSpec(memory_space=pltpu.VMEM)] * len(parts),
        out_specs=[pl.BlockSpec(memory_space=pltpu.VMEM)] * outs,
        out_shape=[shape] * outs,
        compiler_params=limit(8),
        cost_estimate=cost(1),
        name="add_and_cut",
    )(scal, *parts)


def place_kernel(n, scal, *refs):
    pieces, outs = refs[:8], refs[8:]
    for d in range(4):
        y = lax.rem(scal[S_Y] + 4 - d, 4)
        for swapped in range(2):
            core = scal[S_CORE] if swapped == 0 else 1 - scal[S_CORE]
            cols = pl.ds(pl.multiple_of(core * (HALF * DH), HALF * DH), HALF * DH)
            for e in range(4):
                z = lax.rem(scal[S_Z] + 4 - e, 4)
                row = pl.multiple_of(y * 128 + z * 32, 32)
                for k in range(n):
                    outs[k][pl.ds(row, 32), cols] = pieces[2 * d + swapped][e, k]


def place(scal, pieces):
    n = pieces[0].shape[1]
    shape = jax.ShapeDtypeStruct((ROWS, NH * DH), BF16)
    return pl.pallas_call(
        functools.partial(place_kernel, n),
        in_specs=[pl.BlockSpec(memory_space=pltpu.SMEM)] + [pl.BlockSpec(memory_space=pltpu.VMEM)] * 8,
        out_specs=[pl.BlockSpec(memory_space=pltpu.VMEM)] * n,
        out_shape=[shape] * n,
        compiler_params=limit(8),
        cost_estimate=cost(1),
        name="place",
    )(scal, *pieces)


def per_device(vq, vk, vv, vg, aq, ak, av, ag, alignment):
    y, z, core, aud = (lax.axis_index(name) for name in ("y", "z", "core", "aud"))
    vid = (y * 4 + z) * 2 + core
    mask = lax.dynamic_slice(alignment, (vid * 4, 0), (4, 16)).reshape(64)
    scal = jnp.concatenate([jnp.stack([y, z, core, aud]).astype(jnp.int32), mask])

    apart, share_a = statistics(audio_stats_kernel, "audio_stats", scal, vk, vv, aq, ag)
    vpart, share_v = statistics(video_stats_kernel, "video_stats", after(scal, apart), vq, vg, ak, av)
    apart = merge(scal, [after(apart, vpart), swap(apart, "core")], False)
    apart = merge(scal, along(apart, "z"), False)
    vstat = merge(scal, [vpart, swap(vpart, "aud")], True)
    share_v = swap(after(share_v, apart), "aud")
    keep_v, send_v, dvq = own_video(after(scal, apart), vq, vg, ak, av, vstat)
    share_v = after(share_v, dvq)
    astat = merge(scal, along(apart, "y", dvq), True)
    astat_other = swap(astat, "aud")
    share_a = swap(after(share_a, astat), "aud")
    keep_a, send_a, dvk, dvv = own_audio(after(scal, share_v), vk, vv, aq, ag, astat)
    send_a = after(send_a, astat_other, share_a)
    cut = add_and_cut(scal, [[keep_v, swap(send_v, "core")], [keep_a, swap(send_a, "core")]], S_Y)
    share = jnp.concatenate([share_a, after(share_v, cut[0])])
    shards_y = shards(cut, "y")
    cut = add_and_cut(scal, [shards_y], S_Z)
    share = after(share, shards_y[1])
    own, first, third = share, shift(share, "y", 1), shift(share, "y", 3)
    shards_z = shards(cut, "z")
    piece = add_and_cut(scal, [shards_z], None)[0]
    second = shift(after(share, piece), "y", 2)
    line = jnp.stack(along(after(piece, first, third), "z"))
    pieces = both_cores([own, first, after(second, line), third])
    dvq = other_video(after(scal, line), vq, vg, vstat, dvq, pieces)
    dvk, dvv = other_audio(after(scal, dvq), vk, vv, astat_other, dvk, dvv, pieces)
    gathered = along(line, "y")
    gathered = both_cores(gathered[:1]) + both_cores([after(part, dvk) for part in gathered[1:]])
    dak, dav, daq = place(scal, gathered)
    return dvq, dvk, dvv, daq, dak, dav


def solution(mesh):
    grid = Mesh(mesh.devices.reshape(4, 4, 2, 2, 4), ("y", "z", "core", "aud", "head"))
    video = P(("y", "z", "core"), "head")
    audio = P("aud", "head")
    return jax.shard_map(
        per_device,
        mesh=grid,
        in_specs=(video,) * 4 + (audio,) * 4 + (P(),),
        out_specs=(video,) * 3 + (audio,) * 3,
        check_vma=False,
    )
```

```python
import functools
import math

import jax
import jax.numpy as jnp
from jax import lax
from jax.experimental import pallas as pl
from jax.experimental.pallas import tpu as pltpu
from jax.sharding import Mesh
from jax.sharding import PartitionSpec as P

DH = 128
VBLK = 128
ABLK = 64
NH = 6
HALF = 3
ROWS = 512
CH = 256
SHARE = 64
SCALE = DH ** -0.5
C2 = SCALE * math.log2(math.e)
MASKED = -1e30
FLOOR = -1e29
WIDE = HALF * DH
F32 = jnp.float32
BF16 = jnp.bfloat16
STAT = ((3, 8, ROWS), F32)
BOTH = ((2, 8, ROWS), F32)

S_Y, S_Z, S_CORE, S_AUD, S_MASK = 0, 1, 2, 3, 4

MIB = 1024 * 1024


def cost(us):
    return pl.CostEstimate(flops=us * 1_000_000_000, bytes_accessed=100_000, transcendentals=0)


def limit(mib):
    return pltpu.CompilerParams(vmem_limit_bytes=mib * MIB)


def call(kernel, ins, outs, scratch, mib, us, name, scal, *arrays):
    vmem = pl.BlockSpec(memory_space=pltpu.VMEM)
    return pl.pallas_call(
        kernel,
        in_specs=[pl.BlockSpec(memory_space=pltpu.SMEM)] + [vmem] * ins,
        out_specs=[vmem] * len(outs),
        out_shape=[jax.ShapeDtypeStruct(shape, dtype) for shape, dtype in outs],
        scratch_shapes=scratch,
        compiler_params=limit(mib),
        cost_estimate=cost(us),
        name=name,
    )(scal, *arrays)


def dot_nt(a, b):
    return lax.dot_general(a, b, (((1,), (1,)), ((), ())), preferred_element_type=F32)


def dot_nn(a, b):
    return lax.dot_general(a, b, (((1,), (0,)), ((), ())), preferred_element_type=F32)


def bias_of(scal, half, i, j):
    return jnp.where(scal[S_MASK + i * 16 + half * 8 + j] > 0, 0.0, MASKED)


def chunk_active(scal, half, q):
    c = scal[S_Y] * 4 + scal[S_Z]
    first = half * 8 + q * (CH // ABLK)
    return jnp.logical_and(first <= c + 3, first + CH // ABLK - 1 >= c - 3)


def each_chunk(scal, half, body, idle=None):
    @pl.loop(0, ROWS // CH)
    def _(q):
        rows = pl.ds(pl.multiple_of(q * CH, CH), CH)
        active = chunk_active(scal, half, q)

        @pl.when(active)
        def _():
            body(q, rows)

        if idle is not None:

            @pl.when(jnp.logical_not(active))
            def _():
                idle(rows)


def each_head(body, together):
    if together == NH:
        for u in range(NH):
            body(u, u)
        return

    @pl.loop(0, NH // together)
    def _(p):
        for u in range(together):
            body(together * p + u, u)


def pair_bias(scal, half, i, j):
    lane = lax.broadcasted_iota(jnp.int32, (1, 128), 1)
    return jnp.where(lane < ABLK, bias_of(scal, half, i, j), bias_of(scal, half, i, j + 1))


def head_cols(g, r):
    if isinstance(g, int) and isinstance(r, int):
        return slice(g * WIDE + r * DH, g * WIDE + (r + 1) * DH)
    return pl.ds(pl.multiple_of(g * WIDE + r * DH, DH), DH)


def first_rows(held):
    for h in range(NH):
        held[h, 0:1, :] = jnp.full((1, ROWS), FLOOR, F32)
        held[h, 1:2, :] = jnp.zeros((1, ROWS), F32)
        held[h, 2:3, :] = jnp.zeros((1, ROWS), F32)


def store_rows(stat, held):
    for k in range(3):
        for h in range(NH):
            stat[k, h : h + 1, :] = held[h, k : k + 1, :]
        stat[k, NH:8, :] = jnp.ones((8 - NH, ROWS), F32)


def shared_rows(scal):
    return pl.ds(pl.multiple_of(scal[S_Y] * 128 + scal[S_CORE] * SHARE, SHARE), SHARE)


def audio_stats_kernel(scal, vk, vv, aq, ag, stat, share, held):
    half = scal[S_AUD]
    first_rows(held)

    def chunk(q, rows):
        bias = [[pair_bias(scal, half, i, q * 4 + jj * 2) for i in range(4)] for jj in range(2)]

        def head(h, u):
            hc = head_cols(0, h)
            s = dot_nt(vk[:, hc], aq[rows, hc])
            t = dot_nt(vv[:, hc], ag[rows, hc])
            for jj in range(CH // 128):
                cols = slice(jj * 128, (jj + 1) * 128)
                out = pl.ds(pl.multiple_of(q * CH + jj * 128, 128), 128)
                top = jnp.full((1, 128), FLOOR, F32)
                for i in range(4):
                    best = jnp.max(s[i * 128 : (i + 1) * 128, cols], axis=0, keepdims=True)
                    top = jnp.maximum(top, best * C2 + bias[jj][i])
                total = jnp.zeros((1, 128), F32)
                part = jnp.zeros((1, 128), F32)
                for i in range(4):
                    e = jnp.exp2(s[i * 128 : (i + 1) * 128, cols] * C2 - (top - bias[jj][i]))
                    total += jnp.sum(e, axis=0, keepdims=True)
                    part += jnp.sum(e * t[i * 128 : (i + 1) * 128, cols], axis=0, keepdims=True)
                held[h, 0:1, out] = top
                held[h, 1:2, out] = total
                held[h, 2:3, out] = part

        each_head(head, NH)

    each_chunk(scal, half, chunk)
    store_rows(stat, held)
    rows = shared_rows(scal)
    share[0] = aq[rows, :]
    share[1] = ag[rows, :]


def video_stats_kernel(scal, vq, vg, ak, av, audio_share, stat, share, held):
    half = scal[S_AUD]
    first_rows(held)

    def chunk(q, rows):
        bias = [[bias_of(scal, half, i, q * 4 + j) for j in range(4)] for i in range(4)]

        def head(h, u):
            hc = head_cols(0, h)
            s = dot_nt(ak[rows, hc], vq[:, hc])
            t = dot_nt(av[rows, hc], vg[:, hc])
            for i in range(4):
                cols = slice(i * 128, (i + 1) * 128)
                old = held[h, 0:1, cols]
                top = old
                for j in range(4):
                    best = jnp.max(s[j * 64 : (j + 1) * 64, cols], axis=0, keepdims=True)
                    top = jnp.maximum(top, best * C2 + bias[i][j])
                shrink = jnp.exp2(old - top)
                total = held[h, 1:2, cols] * shrink
                part = held[h, 2:3, cols] * shrink
                for j in range(4):
                    e = jnp.exp2(s[j * 64 : (j + 1) * 64, cols] * C2 - (top - bias[i][j]))
                    total += jnp.sum(e, axis=0, keepdims=True)
                    part += jnp.sum(e * t[j * 64 : (j + 1) * 64, cols], axis=0, keepdims=True)
                held[h, 0:1, cols] = top
                held[h, 1:2, cols] = total
                held[h, 2:3, cols] = part

        each_head(head, NH)

    each_chunk(scal, half, chunk)
    store_rows(stat, held)
    rows = shared_rows(scal)
    share[0] = audio_share[0]
    share[1] = ak[rows, :]
    share[2] = av[rows, :]
    share[3] = audio_share[1]


def statistics(kernel, name, shared, scal, *arrays):
    scratch = [pltpu.VMEM((NH, 8, ROWS), F32)]
    share = ((shared, SHARE, NH * DH), BF16)
    return call(kernel, len(arrays), [STAT, share], scratch, 24, 20, name, scal, *arrays)


def merge_kernel(final, scal, *refs):
    *ins, out = refs
    tops = [r[0] for r in ins]
    top = functools.reduce(jnp.maximum, tops)
    weights = [jnp.exp2(t - top) for t in tops]
    total = sum(r[1] * w for r, w in zip(ins, weights))
    part = sum(r[2] * w for r, w in zip(ins, weights))
    if final:
        out[0] = top + jnp.log(total) * math.log2(math.e)
        out[1] = part / total
    else:
        out[0] = top
        out[1] = total
        out[2] = part


def merge(scal, stats, final):
    kernel = functools.partial(merge_kernel, final)
    return call(kernel, len(stats), [BOTH if final else STAT], [], 4, 1, "merge", scal, *stats)[0]


def video_queries(scal, half, q, h, ak, av, vq, vg, vstat, prob, dscore):
    s = dot_nt(ak, vq)
    t = dot_nt(av, vg)
    lses = vstat[0, pl.ds(h, 1), :]
    deltas = vstat[1, pl.ds(h, 1), :]
    for i in range(4):
        cols = slice(i * 128, (i + 1) * 128)
        lse, delta = lses[:, cols], deltas[:, cols]
        for j in range(4):
            rows = slice(j * 64, (j + 1) * 64)
            p = jnp.exp2(s[rows, cols] * C2 - (lse - bias_of(scal, half, i, q * 4 + j)))
            prob[rows, cols] = p.astype(BF16)
            dscore[rows, cols] = (p * (t[rows, cols] - delta) * SCALE).astype(BF16)


def audio_queries(scal, half, q, h, aq, ag, vk, vv, astat, prob, dscore):
    s = dot_nt(vk, aq)
    t = dot_nt(vv, ag)
    lses = astat[0, pl.ds(h, 1), :]
    deltas = astat[1, pl.ds(h, 1), :]
    for jj in range(CH // 128):
        cols = slice(jj * 128, (jj + 1) * 128)
        first, second = slice(jj * 128, jj * 128 + 128), slice(CH + jj * 128, CH + jj * 128 + 128)
        lse = jnp.where(q == 0, lses[:, first], lses[:, second])
        delta = jnp.where(q == 0, deltas[:, first], deltas[:, second])
        for i in range(4):
            rows = slice(i * 128, (i + 1) * 128)
            p = jnp.exp2(s[rows, cols] * C2 - (lse - pair_bias(scal, half, i, q * 4 + jj * 2)))
            prob[rows, cols] = p.astype(BF16)
            dscore[rows, cols] = (p * (t[rows, cols] - delta) * SCALE).astype(BF16)


def own_head(scal, at):
    h = lax.rem(scal[S_CORE] * HALF + at, NH)
    return h, head_cols(0, h), at // HALF, head_cols(0, at % HALF if isinstance(at, int) else lax.rem(at, HALF))


def own_video_kernel(scal, vq, vg, ak, av, vstat, keep, send, dvq, prob, dscore, acc, sums):
    half = scal[S_AUD]
    acc[...] = jnp.zeros_like(acc)

    def chunk(q, rows):
        def head(at, u):
            h, hc, step, sc = own_head(scal, at)
            video_queries(
                scal, half, q, h, ak[rows, hc], av[rows, hc], vq[:, hc], vg[:, hc], vstat, prob.at[u], dscore.at[u]
            )
            ds = dscore[u]
            sums[step, 0, rows, sc] = dot_nn(ds, vq[:, hc]).astype(BF16)
            sums[step, 1, rows, sc] = dot_nn(prob[u], vg[:, hc]).astype(BF16)
            acc[at] += dot_nn(ak[rows, hc].T, ds)

        each_head(head, NH)

    def idle(rows):
        for step in range(2):
            for k in range(2):
                sums[step, k, rows, :] = jnp.zeros((CH, WIDE), BF16)

    each_chunk(scal, half, chunk, idle)
    keep[...] = sums[0]
    send[...] = sums[1]

    @pl.loop(0, NH)
    def _(at):
        dvq[:, own_head(scal, at)[1]] = acc[at].T


def own_audio_kernel(scal, vk, vv, aq, ag, astat, keep, send, dvk, dvv, prob, dscore, sums):
    half = scal[S_AUD]
    dvk[...] = jnp.zeros_like(dvk)
    dvv[...] = jnp.zeros_like(dvv)

    def chunk(q, rows):
        def head(at, u):
            h, hc, step, sc = own_head(scal, at)
            audio_queries(
                scal, half, q, h, aq[rows, hc], ag[rows, hc], vk[:, hc], vv[:, hc], astat, prob.at[u], dscore.at[u]
            )
            ds = dscore[u]
            sums[step, 0, rows, sc] = dot_nn(vk[:, hc].T, ds).T.astype(BF16)
            dvk[:, hc] += dot_nn(ds, aq[rows, hc])
            dvv[:, hc] += dot_nn(prob[u], ag[rows, hc])

        each_head(head, NH)

    def idle(rows):
        for step in range(2):
            sums[step, 0, rows, :] = jnp.zeros((CH, WIDE), BF16)

    each_chunk(scal, half, chunk, idle)
    keep[...] = sums[0]
    send[...] = sums[1]


MINE = (ROWS, NH * DH)


def own_video(scal, vq, vg, ak, av, vstat):
    part = ((2, ROWS, WIDE), BF16)
    scratch = [pltpu.VMEM((NH, CH, ROWS), BF16)] * 2 + [pltpu.VMEM((NH, DH, ROWS), F32)]
    scratch += [pltpu.VMEM((2, 2, ROWS, WIDE), BF16)]
    return call(
        own_video_kernel, 5, [part, part, (MINE, F32)], scratch, 28, 20, "own_video",
        scal, vq, vg, ak, av, vstat,
    )


def own_audio(scal, vk, vv, aq, ag, astat):
    part = ((1, ROWS, WIDE), BF16)
    scratch = [pltpu.VMEM((NH, ROWS, CH), BF16)] * 2 + [pltpu.VMEM((2, 1, ROWS, WIDE), BF16)]
    return call(
        own_audio_kernel, 5, [part, part, (MINE, F32), (MINE, F32)], scratch, 28, 20, "own_audio",
        scal, vk, vv, aq, ag, astat,
    )


def collect(scal, pieces, audio, which):
    for d in range(4):
        y = lax.rem(scal[S_Y] + 4 - d, 4)
        for swapped in range(2):
            core = scal[S_CORE] if swapped == 0 else 1 - scal[S_CORE]
            row = pl.multiple_of(y * 128 + core * SHARE, SHARE)
            for at, k in enumerate(which):
                audio[at, pl.ds(row, SHARE), :] = pieces[2 * d + swapped][k]


def other_video_kernel(scal, vq, vg, vstat, pvq, *refs):
    pieces, (dvq, audio, prob, dscore, acc) = refs[:8], refs[8:]
    half = 1 - scal[S_AUD]
    collect(scal, pieces, audio, (1, 2))
    acc[...] = jnp.zeros_like(acc)

    def chunk(q, rows):
        def head(h, u):
            hc = head_cols(0, h)
            ak, av = audio[0, rows, hc], audio[1, rows, hc]
            video_queries(scal, half, q, h, ak, av, vq[:, hc], vg[:, hc], vstat, prob.at[u], dscore.at[u])
            acc[h] += dot_nn(ak.T, dscore[u])

        each_head(head, 2)

    each_chunk(scal, half, chunk)

    @pl.loop(0, NH)
    def _(h):
        hc = head_cols(0, h)
        dvq[:, hc] = (pvq[:, hc] + acc[h].T).astype(BF16)


def other_audio_kernel(scal, vk, vv, astat, pvk, pvv, *refs):
    pieces, (dvk, dvv, audio, prob, dscore, acck, accv) = refs[:8], refs[8:]
    half = 1 - scal[S_AUD]
    collect(scal, pieces, audio, (0, 3))
    acck[...] = pvk[...]
    accv[...] = pvv[...]

    def chunk(q, rows):
        def head(h, u):
            hc = head_cols(0, h)
            aq, ag = audio[0, rows, hc], audio[1, rows, hc]
            audio_queries(scal, half, q, h, aq, ag, vk[:, hc], vv[:, hc], astat, prob.at[u], dscore.at[u])
            acck[:, hc] += dot_nn(dscore[u], aq)
            accv[:, hc] += dot_nn(prob[u], ag)

        each_head(head, 2)

    each_chunk(scal, half, chunk)
    dvk[...] = acck[...].astype(BF16)
    dvv[...] = accv[...].astype(BF16)


def other_video(scal, vq, vg, vstat, pvq, pieces):
    scratch = [pltpu.VMEM((2,) + MINE, BF16)] + [pltpu.VMEM((2, CH, ROWS), BF16)] * 2
    scratch += [pltpu.VMEM((NH, DH, ROWS), F32)]
    return call(
        other_video_kernel, 12, [(MINE, BF16)], scratch, 28, 20, "other_video",
        scal, vq, vg, vstat, pvq, *pieces,
    )[0]


def other_audio(scal, vk, vv, astat, pvk, pvv, pieces):
    scratch = [pltpu.VMEM((2,) + MINE, BF16)] + [pltpu.VMEM((2, ROWS, CH), BF16)] * 2
    scratch += [pltpu.VMEM(MINE, F32)] * 2
    return call(
        other_audio_kernel, 13, [(MINE, BF16), (MINE, BF16)], scratch, 28, 20, "other_audio",
        scal, vk, vv, astat, pvk, pvv, *pieces,
    )


def shift(x, axis, d):
    return lax.ppermute(x, axis, [(i, (i + d) % 4) for i in range(4)])


def swap(x, axis):
    return lax.ppermute(x, axis, [(0, 1), (1, 0)])


def along(x, axis, held=None):
    return [x if held is None else after(x, held)] + [shift(x, axis, d) for d in (1, 2, 3)]


def shards(cut, axis):
    return [cut[0]] + [shift(cut[d], axis, d) for d in (1, 2, 3)]


def both_cores(parts):
    return [p for part in parts for p in (part, swap(part, "core"))]


def after(x, *others):
    return lax.optimization_barrier((x, *others))[0]


def add_kernel(groups, axis, size, scal, *refs):
    outs = refs[sum(groups) :]
    at = 0
    first = 0
    for count in groups:
        ins = refs[at : at + count]
        n = ins[0].shape[0]
        for d, out in enumerate(outs):
            if size is None:
                rows = slice(None)
            else:
                rows = pl.ds(pl.multiple_of(lax.rem(scal[axis] + d, 4) * size, size), size)
            total = sum(r[:, rows, :].astype(F32) for r in ins)
            out[first : first + n] = total.astype(BF16)
        at += count
        first += n


def add_and_cut(scal, groups, axis):
    parts = [part for group in groups for part in group]
    n = sum(group[0].shape[0] for group in groups)
    _, rows, width = parts[0].shape
    size = None if axis is None else rows // 4
    outs = 1 if axis is None else 4
    shape = jax.ShapeDtypeStruct((n, rows if axis is None else size, width), BF16)
    return pl.pallas_call(
        functools.partial(add_kernel, [len(group) for group in groups], axis, size),
        in_specs=[pl.BlockSpec(memory_space=pltpu.SMEM)] + [pl.BlockSpec(memory_space=pltpu.VMEM)] * len(parts),
        out_specs=[pl.BlockSpec(memory_space=pltpu.VMEM)] * outs,
        out_shape=[shape] * outs,
        compiler_params=limit(8),
        cost_estimate=cost(1),
        name="add_and_cut",
    )(scal, *parts)


def place_kernel(n, scal, *refs):
    pieces, outs = refs[:8], refs[8:]
    for d in range(4):
        y = lax.rem(scal[S_Y] + 4 - d, 4)
        for swapped in range(2):
            core = scal[S_CORE] if swapped == 0 else 1 - scal[S_CORE]
            cols = pl.ds(pl.multiple_of(core * (HALF * DH), HALF * DH), HALF * DH)
            for e in range(4):
                z = lax.rem(scal[S_Z] + 4 - e, 4)
                row = pl.multiple_of(y * 128 + z * 32, 32)
                for k in range(n):
                    outs[k][pl.ds(row, 32), cols] = pieces[2 * d + swapped][e, k]


def place(scal, pieces):
    n = pieces[0].shape[1]
    shape = jax.ShapeDtypeStruct((ROWS, NH * DH), BF16)
    return pl.pallas_call(
        functools.partial(place_kernel, n),
        in_specs=[pl.BlockSpec(memory_space=pltpu.SMEM)] + [pl.BlockSpec(memory_space=pltpu.VMEM)] * 8,
        out_specs=[pl.BlockSpec(memory_space=pltpu.VMEM)] * n,
        out_shape=[shape] * n,
        compiler_params=limit(8),
        cost_estimate=cost(1),
        name="place",
    )(scal, *pieces)


def per_device(vq, vk, vv, vg, aq, ak, av, ag, alignment):
    y, z, core, aud = (lax.axis_index(name) for name in ("y", "z", "core", "aud"))
    vid = (y * 4 + z) * 2 + core
    mask = lax.dynamic_slice(alignment, (vid * 4, 0), (4, 16)).reshape(64)
    scal = jnp.concatenate([jnp.stack([y, z, core, aud]).astype(jnp.int32), mask])

    apart, share = statistics(audio_stats_kernel, "audio_stats", 2, scal, vk, vv, aq, ag)
    vpart, share = statistics(video_stats_kernel, "video_stats", 4, after(scal, apart), vq, vg, ak, av, share)
    apart = merge(scal, [after(apart, vpart), swap(apart, "core")], False)
    apart = merge(scal, along(apart, "z"), False)
    vstat = merge(scal, [vpart, swap(vpart, "aud")], True)
    keep_v, send_v, dvq = own_video(after(scal, apart), vq, vg, ak, av, vstat)
    astat = merge(scal, along(apart, "y", dvq), True)
    share = swap(after(share, astat), "aud")
    astat_other = swap(astat, "aud")
    keep_a, send_a, dvk, dvv = own_audio(scal, vk, vv, aq, ag, astat)
    share = after(share, dvk)
    send_a = after(send_a, astat_other)
    cut = add_and_cut(scal, [[keep_v, swap(send_v, "core")], [keep_a, swap(send_a, "core")]], S_Y)
    shards_y = shards(cut, "y")
    cut = add_and_cut(scal, [shards_y], S_Z)
    share = after(share, shards_y[1])
    own, first, third = share, shift(share, "y", 1), shift(share, "y", 3)
    shards_z = shards(cut, "z")
    piece = add_and_cut(scal, [shards_z], None)[0]
    second = shift(after(share, piece), "y", 2)
    line = jnp.stack(along(after(piece, first, third), "z"))
    pieces = both_cores([own, first, after(second, line), third])
    dvq = other_video(after(scal, line), vq, vg, vstat, dvq, pieces)
    dvk, dvv = other_audio(after(scal, dvq), vk, vv, astat_other, dvk, dvv, pieces)
    gathered = along(line, "y")
    gathered = both_cores(gathered[:1]) + both_cores([after(part, dvk) for part in gathered[1:]])
    dak, dav, daq = place(scal, gathered)
    return dvq, dvk, dvv, daq, dak, dav


def solution(mesh):
    grid = Mesh(mesh.devices.reshape(4, 4, 2, 2, 4), ("y", "z", "core", "aud", "head"))
    video = P(("y", "z", "core"), "head")
    audio = P("aud", "head")
    return jax.shard_map(
        per_device,
        mesh=grid,
        in_specs=(video,) * 4 + (audio,) * 4 + (P(),),
        out_specs=(video,) * 3 + (audio,) * 3,
        check_vma=False,
    )
```
